32 devices in a mesh: case: 2 (over y), mode: 4 (over z), harm: 2 (over x), rad: 2 (over core).
Axes of the slice: x: 2, y: 2, z: 4, core: 2. Of those that a mesh axis runs over, the one named last changes fastest.
Arguments:
- direct_field: bfloat16 [16, 16, 2, 5, 16, 256], P(('case', 'harm'), 'mode', None, None, None, 'rad'), parts along dimension 0, may hold values from -6 to 6
- adjoint_field: bfloat16 [16, 16, 2, 5, 16, 256], P(('case', 'harm'), 'mode', None, None, None, 'rad'), parts along dimension 0, may hold values from -6 to 6
- triad_slots: int32 [16, 4, 2], P('mode'), may hold values from 0 to 3
Outputs:
- sensitivity: float32 [32, 2, 5, 16, 256], P(('case', 'harm'), None, None, 'mode', 'rad'), parts along dimension 0
The draws below stay inside these ranges and needn't reach their ends.
There are 2 independent parts, one for each index of `case`. The reference program is written for one: setup_inputs(seed, part) draws one part's arguments, and reference() takes and returns one part's arrays. A program takes and returns all parts, laid end to end along the dimension named above; an argument that names none is the same for every part. Nothing has to cross between parts.
Inputs may be any that keep to these rules, and one draw needn't show every extreme that they name: triad_slots[m, s, 0] is the slot, within the block of 4 modes holding m, of the adjoint factor; triad_slots[m, s, 1] is the slot of the direct factor within the block s blocks below m's block, counted cyclically over 4 blocks.
All inputs are finite; a program needn't handle non-finite values.
Results may differ from the reference program's by a relative error of at most 0.0003.
Values may be sent and summed in bfloat16 or wider, within the bound.
No kernel may reach another device: no remote copies, remote signals or barrier semaphores. Data moves between devices by JAX's collectives and lax.ppermute only.
A program may use at most 64 MiB of HBM per device.

```python
import math
import jax
import jax.numpy as jnp
from jax import lax

FIELDS = 5
HARMS = 8
MODE_DEV = 4
NX = 16
MODES = 16
STOPS = 4
RADIAL = 256


def with_ends(result, stream_key, least, high):
    longest = result.shape.index(max(result.shape))
    spots = []
    for shift in (0, 1):
        where = [jax.random.randint(jax.random.fold_in(stream_key, axis), (), 0, length) for axis, length in enumerate(result.shape)]
        where[longest] = (where[longest] + shift) % result.shape[longest]
        spots.append(tuple(where))
    return result.at[spots[0]].set(least).at[spots[1]].set(high)


def steps_of(rng, extent, pieces, least, high):
    factor_of, own = 1.0, jax.random.fold_in(rng, 6)
    for dim, parts in pieces:
        heights = jnp.exp(jax.random.uniform(jax.random.fold_in(own, dim), (parts,), jnp.float32, least / len(pieces), high / len(pieces)))
        factor_of = factor_of * jnp.repeat(heights, extent[dim] // parts).reshape([-1 if axis == dim else 1 for axis in range(len(extent))])
    return factor_of


def centred(stream_key, dims, width, reach, pieces=(), kind=jnp.bfloat16):
    level = steps_of(stream_key, dims, pieces, -0.22, 0.18) if pieces else 1.0
    result = jax.random.normal(stream_key, dims, jnp.float32) * width * level
    return jnp.minimum(jnp.maximum(result, -reach), reach).astype(kind)


def setup_inputs(seed: int = 0, part: int = 0) -> dict:
    seeds = jax.random.split(jax.random.key(seed), 4)
    part_keys = jax.random.split(jax.random.fold_in(seeds[3], part), 4)
    return {
        "direct_field": centred(part_keys[0], (HARMS, MODES, 2, FIELDS, NX, RADIAL), 1.0, 6.0, ((0, 2), (1, 4), (5, 2))),
        "adjoint_field": centred(part_keys[1], (HARMS, MODES, 2, FIELDS, NX, RADIAL), 1.0, 6.0, ((0, 2), (1, 4), (5, 2))),
        "triad_slots": with_ends(jax.random.randint(seeds[2], (MODES, STOPS, 2), 0, MODE_DEV), jax.random.fold_in(seeds[2], 1), 0, MODE_DEV - 1).astype(jnp.int32),
    }


def stencil(padded, axis, length):

    def shifted(offset):
        return lax.slice_in_dim(padded, offset, offset + length, axis=axis)
    return (shifted(0) - 8.0 * shifted(1) + 8.0 * shifted(3) - shifted(4)) / 12.0

def derivative(source, axis):
    length = source.shape[axis]
    widths = [(0, 0)] * source.ndim
    widths[axis] = (2, 2)
    return stencil(jnp.pad(source, widths), axis, length)

def conj_product(left_side, right_side):
    left_real = left_side[..., 0, :, :, :]
    left_imag = left_side[..., 1, :, :, :]
    right_real = right_side[..., 0, :, :, :]
    right_imag = right_side[..., 1, :, :, :]
    return jnp.stack([left_real * right_real + left_imag * right_imag, left_real * right_imag - left_imag * right_real], axis=-4)

def triad_term(adjoint, adjoint_axial, adjoint_radial, direct, direct_axial, direct_radial):
    total_sum = conj_product(direct[..., 1:2, :, :], adjoint_axial)
    total_sum = total_sum + conj_product(direct[..., 2:3, :, :], adjoint_radial)
    total_sum = total_sum + conj_product(direct_axial, adjoint[..., 1:2, :, :])
    return total_sum + conj_product(direct_radial, adjoint[..., 2:3, :, :])

def reference(direct_field, adjoint_field, triad_slots):
    direct = direct_field.astype(jnp.float32)
    direct_axial = derivative(direct, 4)
    direct_radial = derivative(direct, 5)
    adjoint = adjoint_field.astype(jnp.float32)
    adjoint_axial = derivative(adjoint, 4)
    adjoint_radial = derivative(adjoint, 5)
    scale = 1.0 / math.sqrt(8.0 * STOPS * HARMS)

    def select(source, position):
        return lax.dynamic_index_in_dim(source, position, axis=1, keepdims=False)

    def one_mode(mode_index):
        block_index = mode_index // MODE_DEV

        def one_stop(running, stop_index):
            slot_pair = triad_slots[mode_index, stop_index]
            adjoint_mode = block_index * MODE_DEV + slot_pair[0]
            direct_mode = (block_index - stop_index) % STOPS * MODE_DEV + slot_pair[1]
            term = triad_term(select(adjoint, adjoint_mode), select(adjoint_axial, adjoint_mode), select(adjoint_radial, adjoint_mode), select(direct, direct_mode), select(direct_axial, direct_mode), select(direct_radial, direct_mode))
            return (running + lax.optimization_barrier(jnp.sum(term, axis=0)), None)
        start_sum = jnp.zeros((2, FIELDS, NX, RADIAL), jnp.float32)
        running, _ = lax.scan(one_stop, start_sum, jnp.arange(STOPS, dtype=jnp.int32))
        return running * scale
    return lax.map(one_mode, jnp.arange(MODES, dtype=jnp.int32))
```

```python
import functools
import math

import jax
import jax.numpy as jnp
from jax import lax
from jax.experimental import pallas as pl
from jax.experimental.pallas import tpu as pltpu
from jax.sharding import PartitionSpec as P

HARMS = 8
LANES = 128
HALO = 4
VMEM_LIMIT = 48 * 1024 * 1024


def iota(shape, axis):
    return lax.broadcasted_iota(jnp.int32, shape, axis)


def one_hot(mask):
    return jnp.where(mask, 1.0, 0.0).astype(jnp.bfloat16)


def halo_offset(index, width):
    return jnp.where(index < 2, index - 2, index - 2 + width)


def pack_kernel(sizes, rad_ref, own_d, own_a, far_d, far_a, out_ref, main_m, halo_m):
    harms, blocks, groups, group_rows, width = sizes
    shift = jnp.where(rad_ref[0] == 0, LANES, -LANES)
    depth, span = harms * LANES, blocks * LANES
    row, col = iota((depth, span), 0), iota((depth, span), 1)
    harm_in, cell_in = row // LANES, row % LANES
    owner, lane = col // LANES, col % LANES
    main_m[...] = one_hot((lane // width == harm_in) & (cell_in == owner * width + lane % width))
    span_h = harms * HALO
    part = lane % span_h
    wanted = owner * width + halo_offset(part % HALO, width)
    same = (part // HALO == harm_in) & (lane < groups * span_h)
    halo_m[0:depth, :] = one_hot(same & (cell_in == wanted))
    halo_m[depth:, :] = one_hot(same & (cell_in + shift == wanted))
    lane_group = (iota((group_rows, span), 1) % LANES) // span_h
    for array, (own, far) in enumerate(((own_d, far_d), (own_a, far_a))):
        held = jnp.zeros((group_rows, span), jnp.float32)
        for group in range(groups):
            rows = slice(group * group_rows, (group + 1) * group_rows)
            near = jnp.concatenate([own[k, rows, :] for k in range(harms)], axis=1)
            both = jnp.concatenate([near] + [far[k, rows, :] for k in range(harms)], axis=1)
            main = jnp.dot(near, main_m[...], preferred_element_type=jnp.float32)
            ends = jnp.dot(both, halo_m[...], preferred_element_type=jnp.float32)
            held = jnp.where(lane_group == group, ends, held)
            for block in range(blocks):
                out_ref[block, array, rows, :] = main[
                    :, block * LANES : (block + 1) * LANES
                ].astype(jnp.bfloat16)
        tail = slice(groups * group_rows, (groups + 1) * group_rows)
        for block in range(blocks):
            out_ref[block, array, tail, :] = held[
                :, block * LANES : (block + 1) * LANES
            ].astype(jnp.bfloat16)


def coefficient(distance):
    near = jnp.where(distance == 1, 8.0, jnp.where(distance == -1, -8.0, 0.0))
    return jnp.where(distance == 2, -1.0, jnp.where(distance == -2, 1.0, near))


def triad_kernel(sizes, slots_ref, in_ref, out_ref, radial_m, axial_m, axial_v, radial_v, sums):
    harms, blocks, groups, group_rows, width, slots, fields, cells, harm_devices = sizes
    span_h = harms * HALO
    used = harms * width
    shape = (LANES, LANES)
    row, col = iota(shape, 0), iota(shape, 1)
    inside = (row // width == col // width) & (row < used) & (col < used)
    radial_m[:, 0:LANES, :] = jnp.broadcast_to(
        jnp.where(inside, coefficient(row - col), 0.0).astype(jnp.bfloat16), (groups, LANES, LANES)
    )
    for group in range(groups):
        part = row - group * span_h
        mine = (part >= 0) & (part < span_h) & (col < used) & (part // HALO == col // width)
        place = halo_offset(part % HALO, width)
        radial_m[group, LANES:, :] = jnp.where(mine, coefficient(place - col % width), 0.0).astype(
            jnp.bfloat16
        )
    square = (group_rows, group_rows)
    row, col = iota(square, 0), iota(square, 1)
    axial_m[...] = jnp.where(row // cells == col // cells, coefficient(col - row), 0.0).astype(
        jnp.bfloat16
    )

    @pl.loop(0, blocks)
    def _(block):
        for array in range(2):
            tail = in_ref[block, array, groups * group_rows :, :]
            for group in range(groups):
                here = in_ref[block, array, group * group_rows : (group + 1) * group_rows, :]
                wide = jnp.concatenate([here, tail], axis=1)
                radial_v[array, block * groups + group] = jnp.dot(
                    wide, radial_m[group], preferred_element_type=jnp.float32
                )
                axial_v[array, block * groups + group] = jnp.dot(
                    axial_m[...], here, preferred_element_type=jnp.float32
                )

    def values(array, block, slot, part, field):
        start = (slot * 2 + part) * group_rows + field * cells
        rows = pl.ds(pl.multiple_of(start, cells), cells)
        return in_ref[block, array, rows, :].astype(jnp.float32)

    @pl.loop(0, blocks * slots)
    def _(mode):
        block = mode // slots

        def add_stop(stop, running):
            adjoint_slot = slots_ref[(mode * blocks + stop) * 2]
            direct_slot = slots_ref[(mode * blocks + stop) * 2 + 1]
            source = lax.rem(block - stop + blocks, blocks)
            at_a = block * groups + adjoint_slot * 2
            at_d = source * groups + direct_slot * 2
            d1r, d1i, d2r, d2i = (
                values(0, source, direct_slot, part, field) for field in (1, 2) for part in (0, 1)
            )
            a1r, a1i, a2r, a2i = (
                values(1, block, adjoint_slot, part, field) for field in (1, 2) for part in (0, 1)
            )
            result = []
            for field in range(fields):
                rows = slice(field * cells, (field + 1) * cells)
                xar, xai = axial_v[1, at_a, rows, :], axial_v[1, at_a + 1, rows, :]
                rar, rai = radial_v[1, at_a, rows, :], radial_v[1, at_a + 1, rows, :]
                xdr, xdi = axial_v[0, at_d, rows, :], axial_v[0, at_d + 1, rows, :]
                rdr, rdi = radial_v[0, at_d, rows, :], radial_v[0, at_d + 1, rows, :]
                real = (d1r * xar + d1i * xai) + (d2r * rar + d2i * rai)
                real = real + ((xdr * a1r + xdi * a1i) + (rdr * a2r + rdi * a2i))
                imag = (d1r * xai - d1i * xar) + (d2r * rai - d2i * rar)
                imag = imag + ((xdr * a1i - xdi * a1r) + (rdr * a2i - rdi * a2r))
                old_real, old_imag = running[field]
                result.append((old_real + real, old_imag + imag))
            return tuple(result)

        zero = jnp.zeros((cells, LANES), jnp.float32)
        running = tuple((zero, zero) for _ in range(fields))
        if blocks <= 4:
            for stop in range(blocks):
                running = add_stop(stop, running)
        else:
            running = lax.fori_loop(0, blocks, add_stop, running)
        for field in range(fields):
            for part in range(2):
                sums[mode, part, field * cells : (field + 1) * cells, :] = running[field][part]

    scale = 1.0 / (12.0 * math.sqrt(8.0 * blocks * HARMS))
    per_harm = blocks // harm_devices
    own_cells = cells // blocks

    @pl.loop(0, blocks)
    def _(block):
        lane_slot = iota((group_rows, LANES), 1) // width
        for part in range(2):
            packed = jnp.zeros((group_rows, LANES), jnp.float32)
            for slot in range(slots):
                value = sums[block * slots + slot, part]
                reach = harms // 2
                while reach:
                    value = value + pltpu.roll(value, reach * width, axis=1)
                    reach //= 2
                if used < LANES and slot:
                    value = pltpu.roll(value, slot * width, axis=1)
                packed = jnp.where(lane_slot == slot, value, packed)
            packed = packed * scale
            for owner in range(blocks):
                for field in range(fields):
                    start = (part * fields + field) * own_cells
                    source = field * cells + owner * own_cells
                    out_ref[
                        owner * harm_devices + block // per_harm,
                        lax.rem(block, per_harm),
                        start : start + own_cells,
                        :,
                    ] = packed[source : source + own_cells, :]


def unpack_kernel(sizes, in_ref, out_ref):
    blocks, harm_devices, slots, width, per_harm = sizes
    rows = in_ref.shape[2]
    lane_block = iota((rows, LANES), 1) // width
    for local in range(per_harm):
        totals = []
        for block in range(blocks):
            total = in_ref[block * harm_devices, local]
            for harm in range(1, harm_devices):
                total = total + in_ref[block * harm_devices + harm, local]
            totals.append(total)
        for slot in range(slots):
            packed = jnp.zeros((rows, LANES), jnp.float32)
            for block in range(blocks):
                amount = (block - slot) * width % LANES
                moved = pltpu.roll(totals[block], amount, axis=1) if amount else totals[block]
                packed = jnp.where(lane_block == block, moved, packed)
            out_ref[local * slots + slot] = packed


def vmem(count):
    return [pl.BlockSpec(memory_space=pltpu.VMEM)] * count


def body(direct_field, adjoint_field, triad_slots):
    blocks, harm_devices = lax.axis_size("mode"), lax.axis_size("harm")
    harms, slots, _, fields, cells, radial = direct_field.shape
    width = radial // blocks
    groups, group_rows = slots * 2, fields * cells
    rows = groups * group_rows
    params = pltpu.CompilerParams(vmem_limit_bytes=VMEM_LIMIT)

    direct = direct_field.reshape(harms, rows, radial)
    adjoint = adjoint_field.reshape(harms, rows, radial)
    swap = [(0, 1), (1, 0)]
    far_direct = lax.ppermute(direct, "rad", swap)
    far_adjoint = lax.ppermute(adjoint, "rad", swap)
    slot_list = lax.all_gather(triad_slots, "mode", axis=0, tiled=True).reshape(-1)
    rad = lax.axis_index("rad").astype(jnp.int32).reshape(1)

    packed = pl.pallas_call(
        functools.partial(pack_kernel, (harms, blocks, groups, group_rows, width)),
        out_shape=jax.ShapeDtypeStruct((blocks, 2, rows + group_rows, LANES), jnp.bfloat16),
        in_specs=[pl.BlockSpec(memory_space=pltpu.SMEM)] + vmem(4),
        out_specs=vmem(1)[0],
        scratch_shapes=[
            pltpu.VMEM((harms * LANES, blocks * LANES), jnp.bfloat16),
            pltpu.VMEM((2 * harms * LANES, blocks * LANES), jnp.bfloat16),
        ],
        compiler_params=params,
    )(rad, direct, adjoint, far_direct, far_adjoint)

    slabs = lax.all_to_all(packed, "mode", split_axis=0, concat_axis=0, tiled=True)

    per_harm, own_cells = blocks // harm_devices, cells // blocks
    sizes = (harms, blocks, groups, group_rows, width, slots, fields, cells, harm_devices)
    out_rows = 2 * fields * own_cells
    parts = pl.pallas_call(
        functools.partial(triad_kernel, sizes),
        out_shape=jax.ShapeDtypeStruct(
            (blocks * harm_devices, per_harm, out_rows, LANES), jnp.float32
        ),
        in_specs=[pl.BlockSpec(memory_space=pltpu.SMEM)] + vmem(1),
        out_specs=vmem(1)[0],
        scratch_shapes=[
            pltpu.VMEM((groups, 2 * LANES, LANES), jnp.bfloat16),
            pltpu.VMEM((group_rows, group_rows), jnp.bfloat16),
            pltpu.VMEM((2, blocks * groups, group_rows, LANES), jnp.float32),
            pltpu.VMEM((2, blocks * groups, group_rows, LANES), jnp.float32),
            pltpu.VMEM((blocks * slots, 2, group_rows, LANES), jnp.float32),
        ],
        compiler_params=params,
    )(slot_list, slabs)

    owned = lax.all_to_all(parts, ("mode", "harm"), split_axis=0, concat_axis=0, tiled=True)

    result = pl.pallas_call(
        functools.partial(unpack_kernel, (blocks, harm_devices, slots, width, per_harm)),
        out_shape=jax.ShapeDtypeStruct((per_harm * slots, out_rows, LANES), jnp.float32),
        in_specs=vmem(1),
        out_specs=vmem(1)[0],
        compiler_params=params,
    )(owned)
    return result.reshape(per_harm * slots, 2, fields, own_cells, radial)


def solution(mesh):
    return jax.shard_map(
        body,
        mesh=mesh,
        in_specs=(
            P(("case", "harm"), "mode", None, None, None, "rad"),
            P(("case", "harm"), "mode", None, None, None, "rad"),
            P("mode", None, None),
        ),
        out_specs=P(("case", "harm"), None, None, "mode", "rad"),
        check_vma=False,
    )
```

```python
import functools
import math

import jax
import jax.numpy as jnp
from jax import lax
from jax.experimental import pallas as pl
from jax.experimental.pallas import tpu as pltpu
from jax.sharding import PartitionSpec as P

HARMS = 8
LANES = 128
HALO = 4
GROUPS = ((1, 2), (0, 3), (4,))
VMEM_LIMIT = 40 * 1024 * 1024


def iota(shape, axis):
    return lax.broadcasted_iota(jnp.int32, shape, axis)


def one_hot(mask):
    return jnp.where(mask, 1.0, 0.0).astype(jnp.bfloat16)


def halo_offset(index, width):
    return jnp.where(index < 2, index - 2, index - 2 + width)


def wrapped(index, count):
    return jnp.where(index >= count, index - count, index)


def columns(harms, blocks, mode):
    shape = (harms * LANES, blocks * LANES)
    row, col = iota(shape, 0), iota(shape, 1)
    owner = wrapped(col // LANES + mode, blocks)
    return row // LANES, row % LANES, owner, col % LANES


def side_by_side(ref, group, rows):
    return jnp.concatenate([ref[k, group, rows, :] for k in range(ref.shape[0])], axis=1)


def fill_main(matrix, sizes, mode):
    harms, blocks, width = sizes
    harm_in, cell_in, owner, lane = columns(harms, blocks, mode)
    matrix[...] = one_hot(
        (lane // width == harm_in) & (cell_in == owner * width + lane % width)
    )


def write_main(arrays, fields, cells, matrix, outs):
    groups = arrays[0].shape[1]
    pieces = []
    for array in arrays:
        for field in fields:
            rows = slice(field * cells, (field + 1) * cells)
            pieces += [side_by_side(array, group, rows) for group in range(groups)]
    main = jnp.dot(
        jnp.concatenate(pieces, axis=0), matrix[...], preferred_element_type=jnp.float32
    )
    for step, out in enumerate(outs):
        out[...] = main[:, step * LANES : (step + 1) * LANES].astype(jnp.bfloat16)


def first_pack_kernel(sizes, cells, where, *refs):
    blocks = sizes[1]
    fields = len(GROUPS[0])
    ins, outs, matrix = refs[: 2 * fields], refs[2 * fields : -1], refs[-1]
    fill_main(matrix, sizes, where[0])
    groups = ins[0].shape[1]
    pieces = [
        side_by_side(ref, group, slice(0, cells)) for ref in ins for group in range(groups)
    ]
    main = jnp.dot(
        jnp.concatenate(pieces, axis=0), matrix[...], preferred_element_type=jnp.float32
    )
    for step in range(blocks):
        outs[step][...] = main[:, step * LANES : (step + 1) * LANES].astype(jnp.bfloat16)


def second_pack_kernel(sizes, cells, where, own_d, own_a, far_d, far_a, *refs):
    harms, blocks, width = sizes
    outs, main_m, halo_m = refs[:-2], refs[-2], refs[-1]
    groups, group_rows = own_d.shape[1], own_d.shape[2]
    mode = where[0]
    shift = jnp.where(where[2] == 0, LANES, -LANES)
    depth = harms * LANES
    span_h = harms * HALO
    harm_in, cell_in, owner, lane = columns(harms, blocks, mode)
    part = lane % span_h
    wanted = owner * width + halo_offset(part % HALO, width)
    same = (part // HALO == harm_in) & (lane < groups * span_h)
    halo_m[0:depth, :] = one_hot(same & (cell_in == wanted))
    halo_m[depth:, :] = one_hot(same & (cell_in + shift == wanted))
    lane_group = (iota((group_rows, blocks * LANES), 1) % LANES) // span_h
    everything = slice(0, group_rows)
    for array, (own, far) in enumerate(((own_d, far_d), (own_a, far_a))):
        pieces = [
            jnp.concatenate(
                [side_by_side(own, group, everything), side_by_side(far, group, everything)], axis=1
            )
            for group in range(groups)
        ]
        ends = jnp.dot(
            jnp.concatenate(pieces, axis=0), halo_m[...], preferred_element_type=jnp.float32
        )
        held = jnp.zeros((group_rows, blocks * LANES), jnp.float32)
        for group in range(groups):
            held = jnp.where(
                lane_group == group, ends[group * group_rows : (group + 1) * group_rows], held
            )
        for step in range(blocks):
            outs[step][array * group_rows : (array + 1) * group_rows, :] = held[
                :, step * LANES : (step + 1) * LANES
            ].astype(jnp.bfloat16)
    fill_main(main_m, sizes, mode)
    for index, fields in enumerate(GROUPS[1:], start=1):
        write_main(
            (own_d, own_a), fields, cells, main_m, outs[index * blocks : (index + 1) * blocks]
        )


def coefficient(distance):
    near = jnp.where(distance == 1, 8.0, jnp.where(distance == -1, -8.0, 0.0))
    return jnp.where(distance == 2, -1.0, jnp.where(distance == -2, 1.0, near))


def triad_kernel(sizes, fields, where, slots_ref, *refs):
    harms, blocks, width, groups, slots, all_fields, cells, harm_devices = sizes
    first = fields == GROUPS[0]
    lead = refs[:blocks]
    mains = lead if first else refs[blocks : 2 * blocks]
    at = blocks if first else 2 * blocks
    halos = refs[at : at + blocks]
    outs = refs[at + blocks : at + blocks + blocks * harm_devices]
    radial_m, axial_m, plain_v, axial_v, radial_v, sums, staged = refs[
        at + blocks + blocks * harm_devices :
    ]
    count = len(fields)
    span_h = harms * HALO
    used = harms * width
    tile = groups * cells
    shape = (LANES, LANES)
    row, col = iota(shape, 0), iota(shape, 1)
    inside = (row // width == col // width) & (row < used) & (col < used)
    within = jnp.where(inside, coefficient(row - col), 0.0).astype(jnp.bfloat16)
    square = (tile, tile)
    row_t, col_t = iota(square, 0), iota(square, 1)
    axial_m[...] = jnp.where(
        row_t // cells == col_t // cells, coefficient(col_t - row_t), 0.0
    ).astype(jnp.bfloat16)

    for group in range(groups):
        part = row - group * span_h
        mine = (part >= 0) & (part < span_h) & (col < used) & (part // HALO == col // width)
        place = halo_offset(part % HALO, width)
        around = jnp.where(mine, coefficient(place - col % width), 0.0).astype(jnp.bfloat16)
        radial_m[group] = jnp.concatenate([within, around], axis=0)
    for group in range(groups):
        pieces = []
        for array in range(2):
            for local, field in enumerate(fields):
                for step in range(blocks):
                    start = ((array * count + local) * groups + group) * cells
                    beside = (array * all_fields + field) * cells
                    pieces.append(
                        jnp.concatenate(
                            [
                                mains[step][start : start + cells, :],
                                halos[step][beside : beside + cells, :],
                            ],
                            axis=1,
                        )
                    )
        slopes = jnp.dot(
            jnp.concatenate(pieces, axis=0), radial_m[group], preferred_element_type=jnp.float32
        )
        index = 0
        for array in range(2):
            for local in range(count):
                for step in range(blocks):
                    radial_v[array * count + local, step * groups + group] = slopes[
                        index * cells : (index + 1) * cells, :
                    ]
                    index += 1
    for step in range(blocks):
        for local in range(count):
            starts = [(array * count + local) * tile for array in range(2)]
            both = jnp.concatenate([mains[step][s : s + tile, :] for s in starts], axis=1)
            slopes = jnp.dot(axial_m[...], both, preferred_element_type=jnp.float32)
            for array in range(2):
                for group in range(groups):
                    axial_v[array * count + local, step * groups + group] = slopes[
                        group * cells : (group + 1) * cells, array * LANES : (array + 1) * LANES
                    ]
        for which in range(4):
            for group in range(groups):
                start = (which * groups + group) * cells
                plain_v[which, step * groups + group] = lead[step][
                    start : start + cells, :
                ].astype(jnp.float32)

    @pl.loop(0, blocks * slots)
    def _(index):
        step = index // slots

        def add_stop(stop, running):
            source = wrapped(step + stop, blocks)
            at_a = step * groups + slots_ref[(index * blocks + stop) * 2] * 2
            at_d = source * groups + slots_ref[(index * blocks + stop) * 2 + 1] * 2
            d1r, d1i, d2r, d2i = (plain_v[w, at_d + c] for w in (0, 1) for c in (0, 1))
            a1r, a1i, a2r, a2i = (plain_v[w, at_a + c] for w in (2, 3) for c in (0, 1))
            result = []
            for local in range(count):
                xar, xai = axial_v[count + local, at_a], axial_v[count + local, at_a + 1]
                rar, rai = radial_v[count + local, at_a], radial_v[count + local, at_a + 1]
                xdr, xdi = axial_v[local, at_d], axial_v[local, at_d + 1]
                rdr, rdi = radial_v[local, at_d], radial_v[local, at_d + 1]
                real = (d1r * xar + d1i * xai) + (d2r * rar + d2i * rai)
                real = real + ((xdr * a1r + xdi * a1i) + (rdr * a2r + rdi * a2i))
                imag = (d1r * xai - d1i * xar) + (d2r * rai - d2i * rar)
                imag = imag + ((xdr * a1i - xdi * a1r) + (rdr * a2i - rdi * a2r))
                old_real, old_imag = running[local]
                result.append((old_real + real, old_imag + imag))
            return tuple(result)

        zero = jnp.zeros((cells, LANES), jnp.float32)
        running = tuple((zero, zero) for _ in range(count))
        if blocks <= 4:
            for stop in range(blocks):
                running = add_stop(stop, running)
        else:
            running = lax.fori_loop(0, blocks, add_stop, running)
        for local in range(count):
            for part in range(2):
                sums[index, part * count + local] = running[local][part]

    scale = 1.0 / (12.0 * math.sqrt(8.0 * blocks * HARMS))
    per_harm = blocks // harm_devices
    own_cells = cells // blocks
    lane_slot = iota((cells, LANES), 1) // width

    @pl.loop(0, blocks)
    def _(step):
        block = wrapped(where[0] - step + blocks, blocks)
        for row in range(2 * count):
            packed = jnp.zeros((cells, LANES), jnp.float32)
            for slot in range(slots):
                value = sums[step * slots + slot, row]
                reach = harms // 2
                while reach:
                    value = value + pltpu.roll(value, reach * width, axis=1)
                    reach //= 2
                if used < LANES and slot:
                    value = pltpu.roll(value, slot * width, axis=1)
                packed = jnp.where(lane_slot == slot, value, packed)
            packed = packed * scale
            for owner in range(blocks):
                staged[owner, block, row * own_cells : (row + 1) * own_cells, :] = packed[
                    owner * own_cells : (owner + 1) * own_cells, :
                ]

    for step in range(blocks):
        owner = wrapped(where[0] + step, blocks)
        for turn in range(harm_devices):
            harm = wrapped(where[1] + turn, harm_devices)
            for local in range(per_harm):
                outs[step * harm_devices + turn][local] = staged[owner, harm * per_harm + local]


def unpack_kernel(sizes, where, *refs):
    blocks, harm_devices, slots, width, per_harm, own_cells, all_fields = sizes
    ins, out_ref = refs[:-1], refs[-1]
    peers = blocks * harm_devices
    for index, fields in enumerate(GROUPS):
        count = len(fields)
        rows = 2 * count * own_cells
        lane_block = iota((rows, LANES), 1) // width
        for local in range(per_harm):
            packed = [jnp.zeros((rows, LANES), jnp.float32) for _ in range(slots)]
            for step in range(blocks):
                source = wrapped(where[0] - step + blocks, blocks)
                total = ins[index * peers + step * harm_devices][local]
                for turn in range(1, harm_devices):
                    total = total + ins[index * peers + step * harm_devices + turn][local]
                for slot in range(slots):
                    amount = lax.rem((source - slot + blocks) * width, LANES)
                    moved = pltpu.roll(total, amount, axis=1)
                    packed[slot] = jnp.where(lane_block == source, moved, packed[slot])
            for slot in range(slots):
                for part in range(2):
                    for at, field in enumerate(fields):
                        start = (part * count + at) * own_cells
                        target = (part * all_fields + field) * own_cells
                        out_ref[local * slots + slot, target : target + own_cells, :] = packed[
                            slot
                        ][start : start + own_cells, :]


def smem(count):
    return [pl.BlockSpec(memory_space=pltpu.SMEM)] * count


def vmem(count):
    return [pl.BlockSpec(memory_space=pltpu.VMEM)] * count


def moved_up(values, axis):
    count = lax.axis_size(axis)
    result = [values[0]]
    for step in range(1, count):
        pairs = [(source, (source + step) % count) for source in range(count)]
        result.append(lax.ppermute(values[step], axis, pairs))
    return result


def to_owners(parts, mode, harm):
    modes, harms = lax.axis_size("mode"), lax.axis_size("harm")
    if modes * harms > 8:
        stacked = jnp.stack(parts).reshape((modes, harms) + parts[0].shape)
        stacked = jnp.roll(stacked, (mode, harm), axis=(0, 1)).reshape((-1,) + parts[0].shape)
        came = lax.all_to_all(stacked, ("mode", "harm"), split_axis=0, concat_axis=0, tiled=True)
        came = came.reshape((modes, harms) + parts[0].shape)
        came = jnp.take(came, (mode - jnp.arange(modes)) % modes, axis=0)
        came = jnp.take(came, (harm - jnp.arange(harms)) % harms, axis=1)
        return [came[step, turn] for step in range(modes) for turn in range(harms)]
    result = [parts[0]]
    for index in range(1, modes * harms):
        step, turn = divmod(index, harms)
        pairs = [
            (z * harms + h, (z + step) % modes * harms + (h + turn) % harms)
            for z in range(modes)
            for h in range(harms)
        ]
        result.append(lax.ppermute(parts[index], ("mode", "harm"), pairs))
    return result


def body(direct_field, adjoint_field, triad_slots):
    blocks, harm_devices = lax.axis_size("mode"), lax.axis_size("harm")
    harms, slots, parts, fields, cells, radial = direct_field.shape
    width = radial // blocks
    groups, group_rows = slots * parts, fields * cells
    tile = groups * cells
    params = pltpu.CompilerParams(vmem_limit_bytes=VMEM_LIMIT)
    mode, harm, rad = (lax.axis_index(axis).astype(jnp.int32) for axis in ("mode", "harm", "rad"))
    where = jnp.stack([mode, harm, rad])

    direct = direct_field.reshape(harms, groups, group_rows, radial)
    adjoint = adjoint_field.reshape(harms, groups, group_rows, radial)
    swap = [(0, 1), (1, 0)]
    far_direct = lax.ppermute(direct, "rad", swap)
    far_adjoint = lax.ppermute(adjoint, "rad", swap)

    def payload(rows):
        return [jax.ShapeDtypeStruct((rows, LANES), jnp.bfloat16)] * blocks

    def one_field(field):
        return pl.BlockSpec((harms, groups, cells, radial), lambda i: (0, 0, field, 0))

    sizes = (harms, blocks, width)
    main_matrix = pltpu.VMEM((harms * LANES, blocks * LANES), jnp.bfloat16)
    lead = pl.pallas_call(
        functools.partial(first_pack_kernel, sizes, cells),
        grid=(1,),
        out_shape=payload(2 * len(GROUPS[0]) * tile),
        in_specs=smem(1) + [one_field(field) for field in GROUPS[0]] * 2,
        out_specs=vmem(blocks),
        scratch_shapes=[main_matrix],
        compiler_params=params,
        name="pack_first",
    )(where, *[direct] * len(GROUPS[0]), *[adjoint] * len(GROUPS[0]))
    lead = moved_up(lead, "mode")

    shapes = payload(2 * group_rows)
    for group in GROUPS[1:]:
        shapes = shapes + payload(2 * len(group) * tile)
    packed = pl.pallas_call(
        functools.partial(second_pack_kernel, sizes, cells),
        out_shape=shapes,
        in_specs=smem(1) + vmem(4),
        out_specs=vmem(len(shapes)),
        scratch_shapes=[
            main_matrix,
            pltpu.VMEM((2 * harms * LANES, blocks * LANES), jnp.bfloat16),
        ],
        compiler_params=params,
        name="pack_rest",
    )(where, direct, adjoint, far_direct, far_adjoint)
    halos = moved_up(packed[:blocks], "mode")
    mains = [lead]
    for index in range(1, len(GROUPS)):
        mains.append(moved_up(packed[index * blocks : (index + 1) * blocks], "mode"))
    own_slots = triad_slots.reshape(-1)
    slot_list = jnp.concatenate(moved_up([own_slots] * blocks, "mode"))

    per_harm, own_cells = blocks // harm_devices, cells // blocks
    sizes = (harms, blocks, width, groups, slots, fields, cells, harm_devices)
    owned = []
    for index, group in enumerate(GROUPS):
        count = len(group)
        operands = mains[0] + (mains[index] if index else []) + halos
        derived = pltpu.VMEM((2 * count, blocks * groups, cells, LANES), jnp.float32)
        chunk = jax.ShapeDtypeStruct((per_harm, 2 * count * own_cells, LANES), jnp.float32)
        sent = pl.pallas_call(
            functools.partial(triad_kernel, sizes, group),
            out_shape=[chunk] * (blocks * harm_devices),
            in_specs=smem(2) + vmem(len(operands)),
            out_specs=vmem(blocks * harm_devices),
            scratch_shapes=[
                pltpu.VMEM((groups, 2 * LANES, LANES), jnp.bfloat16),
                pltpu.VMEM((tile, tile), jnp.bfloat16),
                pltpu.VMEM((4, blocks * groups, cells, LANES), jnp.float32),
                derived,
                derived,
                pltpu.VMEM((blocks * slots, 2 * count, cells, LANES), jnp.float32),
                pltpu.VMEM((blocks, blocks, 2 * count * own_cells, LANES), jnp.float32),
            ],
            compiler_params=params,
            name="triads",
        )(where, slot_list, *operands)
        owned += to_owners(sent, mode, harm)

    sizes = (blocks, harm_devices, slots, width, per_harm, own_cells, fields)
    result = pl.pallas_call(
        functools.partial(unpack_kernel, sizes),
        out_shape=jax.ShapeDtypeStruct(
            (per_harm * slots, 2 * fields * own_cells, LANES), jnp.float32
        ),
        in_specs=smem(1) + vmem(len(owned)),
        out_specs=vmem(1)[0],
        compiler_params=params,
        name="unpack",
    )(where, *owned)
    return result.reshape(per_harm * slots, 2, fields, own_cells, radial)


def solution(mesh):
    return jax.shard_map(
        body,
        mesh=mesh,
        in_specs=(
            P(("case", "harm"), "mode", None, None, None, "rad"),
            P(("case", "harm"), "mode", None, None, None, "rad"),
            P("mode", None, None),
        ),
        out_specs=P(("case", "harm"), None, None, "mode", "rad"),
        check_vma=False,
    )
```

```python
import functools
import math

import jax
import jax.numpy as jnp
from jax import lax
from jax.experimental import pallas as pl
from jax.experimental.pallas import tpu as pltpu
from jax.sharding import PartitionSpec as P

HARMS = 8
LANES = 128
HALO = 4
SLOT_ROWS = 16
GROUPS = ((1, 2, 0, 3, 4),)
VMEM_LIMIT = 40 * 1024 * 1024


def iota(shape, axis):
    return lax.broadcasted_iota(jnp.int32, shape, axis)


def one_hot(mask):
    return jnp.where(mask, 1.0, 0.0).astype(jnp.bfloat16)


def halo_offset(index, width):
    return jnp.where(index < 2, index - 2, index - 2 + width)


def wrapped(index, count):
    return jnp.where(index >= count, index - count, index)


def columns(harms, blocks):
    shape = (harms * LANES, blocks * LANES)
    row, col = iota(shape, 0), iota(shape, 1)
    return row // LANES, row % LANES, col // LANES, col % LANES


def side_by_side(ref, group, rows):
    return jnp.concatenate([ref[k, group, rows, :] for k in range(ref.shape[0])], axis=1)


def fill_main(matrix, sizes):
    harms, blocks, width = sizes
    harm_in, cell_in, owner, lane = columns(harms, blocks)
    matrix[...] = one_hot(
        (lane // width == harm_in) & (cell_in == owner * width + lane % width)
    )


def write_main(arrays, fields, cells, matrix, out):
    groups = arrays[0].shape[1]
    pieces = []
    for array in arrays:
        for field in fields:
            rows = slice(field * cells, (field + 1) * cells)
            pieces += [side_by_side(array, group, rows) for group in range(groups)]
    main = jnp.dot(
        jnp.concatenate(pieces, axis=0), matrix[...], preferred_element_type=jnp.float32
    )
    for owner in range(out.shape[0]):
        out[owner, 0 : main.shape[0], :] = main[:, owner * LANES : (owner + 1) * LANES].astype(
            jnp.bfloat16
        )


def first_pack_kernel(sizes, cells, rad, slots, own_d, own_a, far_d, far_a, out, main_m, halo_m):
    harms, blocks, width = sizes
    groups, group_rows = own_d.shape[1], own_d.shape[2]
    fill_main(main_m, sizes)
    write_main((own_d, own_a), GROUPS[0], cells, main_m, out)
    base = 2 * len(GROUPS[0]) * groups * cells
    shift = jnp.where(rad[0] == 0, LANES, -LANES)
    depth = harms * LANES
    span_h = harms * HALO
    harm_in, cell_in, owner, lane = columns(harms, blocks)
    part = lane % span_h
    wanted = owner * width + halo_offset(part % HALO, width)
    same = (part // HALO == harm_in) & (lane < groups * span_h)
    halo_m[0:depth, :] = one_hot(same & (cell_in == wanted))
    halo_m[depth:, :] = one_hot(same & (cell_in + shift == wanted))
    lane_group = (iota((group_rows, blocks * LANES), 1) % LANES) // span_h
    everything = slice(0, group_rows)
    for array, (own, far) in enumerate(((own_d, far_d), (own_a, far_a))):
        pieces = [
            jnp.concatenate(
                [side_by_side(own, group, everything), side_by_side(far, group, everything)], axis=1
            )
            for group in range(groups)
        ]
        ends = jnp.dot(
            jnp.concatenate(pieces, axis=0), halo_m[...], preferred_element_type=jnp.float32
        )
        held = jnp.zeros((group_rows, blocks * LANES), jnp.float32)
        for group in range(groups):
            held = jnp.where(
                lane_group == group, ends[group * group_rows : (group + 1) * group_rows], held
            )
        start = base + array * group_rows
        for block in range(blocks):
            out[block, start : start + group_rows, :] = held[
                :, block * LANES : (block + 1) * LANES
            ].astype(jnp.bfloat16)
    lane = iota((SLOT_ROWS, LANES), 1)
    listed = jnp.zeros((SLOT_ROWS, LANES), jnp.int32)
    for index in range(slots.shape[0]):
        listed = jnp.where(lane == index, slots[index], listed)
    start = base + 2 * group_rows
    for block in range(blocks):
        out[block, start : start + SLOT_ROWS, :] = listed.astype(jnp.float32).astype(jnp.bfloat16)


def rest_pack_kernel(sizes, cells, own_d, own_a, *refs):
    outs, matrix = refs[:-1], refs[-1]
    fill_main(matrix, sizes)
    for fields, out in zip(GROUPS[1:], outs):
        write_main((own_d, own_a), fields, cells, matrix, out)


def coefficient(distance):
    near = jnp.where(distance == 1, 8.0, jnp.where(distance == -1, -8.0, 0.0))
    return jnp.where(distance == 2, -1.0, jnp.where(distance == -2, 1.0, near))


def triad_kernel(sizes, fields, *refs):
    harms, blocks, width, groups, slots, all_fields, cells, harm_devices = sizes
    first = fields == GROUPS[0]
    lead, main = refs[0], refs[0 if first else 1]
    at = 1 if first else 2
    out, radial_m, axial_m, plain_v, axial_v, radial_v, sums, slots_v, slots_s, slots_sem = refs[at:]
    halo_row = 2 * len(GROUPS[0]) * groups * cells
    slot_row = halo_row + 2 * all_fields * cells
    for block in range(blocks):
        slots_v[block : block + 1, :] = (
            lead[block, slot_row : slot_row + SLOT_ROWS, :].astype(jnp.float32)[0:1, :]
        ).astype(jnp.int32)
    listing = pltpu.make_async_copy(slots_v, slots_s, slots_sem)
    listing.start()
    count = len(fields)
    span_h = harms * HALO
    used = harms * width
    tile = groups * cells
    shape = (LANES, LANES)
    row, col = iota(shape, 0), iota(shape, 1)
    inside = (row // width == col // width) & (row < used) & (col < used)
    within = jnp.where(inside, coefficient(row - col), 0.0).astype(jnp.bfloat16)
    square = (tile, tile)
    row_t, col_t = iota(square, 0), iota(square, 1)
    axial_m[...] = jnp.where(
        row_t // cells == col_t // cells, coefficient(col_t - row_t), 0.0
    ).astype(jnp.bfloat16)

    for group in range(groups):
        part = row - group * span_h
        mine = (part >= 0) & (part < span_h) & (col < used) & (part // HALO == col // width)
        place = halo_offset(part % HALO, width)
        around = jnp.where(mine, coefficient(place - col % width), 0.0).astype(jnp.bfloat16)
        radial_m[group] = jnp.concatenate([within, around], axis=0)
    for group in range(groups):
        pieces = []
        for array in range(2):
            for local, field in enumerate(fields):
                for step in range(blocks):
                    start = ((array * count + local) * groups + group) * cells
                    beside = halo_row + (array * all_fields + field) * cells
                    pieces.append(
                        jnp.concatenate(
                            [
                                main[step, start : start + cells, :],
                                lead[step, beside : beside + cells, :],
                            ],
                            axis=1,
                        )
                    )
        slopes = jnp.dot(
            jnp.concatenate(pieces, axis=0), radial_m[group], preferred_element_type=jnp.float32
        )
        index = 0
        for array in range(2):
            for local in range(count):
                for step in range(blocks):
                    radial_v[array * count + local, step * groups + group] = slopes[
                        index * cells : (index + 1) * cells, :
                    ]
                    index += 1
    for step in range(blocks):
        for local in range(count):
            starts = [(array * count + local) * tile for array in range(2)]
            both = jnp.concatenate([main[step, s : s + tile, :] for s in starts], axis=1)
            slopes = jnp.dot(axial_m[...], both, preferred_element_type=jnp.float32)
            for array in range(2):
                for group in range(groups):
                    axial_v[array * count + local, step * groups + group] = slopes[
                        group * cells : (group + 1) * cells, array * LANES : (array + 1) * LANES
                    ]
        for which in range(4):
            for group in range(groups):
                held = which // 2 * len(GROUPS[0]) + which % 2
                start = (held * groups + group) * cells
                plain_v[which, step * groups + group] = lead[
                    step, start : start + cells, :
                ].astype(jnp.float32)

    listing.wait()

    @pl.loop(0, blocks * slots)
    def _(index):
        step = index // slots
        entry = lax.rem(index, slots) * blocks

        def add_stop(stop, running):
            source = wrapped(step - stop + blocks, blocks)
            at_a = step * groups + slots_s[step, (entry + stop) * 2] * 2
            at_d = source * groups + slots_s[step, (entry + stop) * 2 + 1] * 2
            d1r, d1i, d2r, d2i = (plain_v[w, at_d + c] for w in (0, 1) for c in (0, 1))
            a1r, a1i, a2r, a2i = (plain_v[w, at_a + c] for w in (2, 3) for c in (0, 1))
            result = []
            for local in range(count):
                xar, xai = axial_v[count + local, at_a], axial_v[count + local, at_a + 1]
                rar, rai = radial_v[count + local, at_a], radial_v[count + local, at_a + 1]
                xdr, xdi = axial_v[local, at_d], axial_v[local, at_d + 1]
                rdr, rdi = radial_v[local, at_d], radial_v[local, at_d + 1]
                real = (d1r * xar + d1i * xai) + (d2r * rar + d2i * rai)
                real = real + ((xdr * a1r + xdi * a1i) + (rdr * a2r + rdi * a2i))
                imag = (d1r * xai - d1i * xar) + (d2r * rai - d2i * rar)
                imag = imag + ((xdr * a1i - xdi * a1r) + (rdr * a2i - rdi * a2r))
                old_real, old_imag = running[local]
                result.append((old_real + real, old_imag + imag))
            return tuple(result)

        zero = jnp.zeros((cells, LANES), jnp.float32)
        running = tuple((zero, zero) for _ in range(count))
        if blocks <= 4:
            for stop in range(blocks):
                running = add_stop(stop, running)
        else:
            running = lax.fori_loop(0, blocks, add_stop, running)
        for local in range(count):
            for part in range(2):
                sums[index, part * count + local] = running[local][part]

    scale = 1.0 / (12.0 * math.sqrt(8.0 * blocks * HARMS))
    per_harm = blocks // harm_devices
    own_cells = cells // blocks
    lane_slot = iota((cells, LANES), 1) // width

    @pl.loop(0, blocks)
    def _(step):
        for row in range(2 * count):
            packed = jnp.zeros((cells, LANES), jnp.float32)
            for slot in range(slots):
                value = sums[step * slots + slot, row]
                reach = harms // 2
                while reach:
                    value = value + pltpu.roll(value, reach * width, axis=1)
                    reach //= 2
                if used < LANES and slot:
                    value = pltpu.roll(value, slot * width, axis=1)
                packed = jnp.where(lane_slot == slot, value, packed)
            packed = packed * scale
            for owner in range(blocks):
                out[
                    owner * harm_devices + step // per_harm,
                    lax.rem(step, per_harm),
                    row * own_cells : (row + 1) * own_cells,
                    :,
                ] = packed[owner * own_cells : (owner + 1) * own_cells, :]


def unpack_kernel(sizes, *refs):
    blocks, harm_devices, slots, width, per_harm, own_cells, all_fields = sizes
    ins, out_ref = refs[:-1], refs[-1]
    for came, fields in zip(ins, GROUPS):
        count = len(fields)
        rows = 2 * count * own_cells
        lane_block = iota((rows, LANES), 1) // width
        for local in range(per_harm):
            packed = [jnp.zeros((rows, LANES), jnp.float32) for _ in range(slots)]
            for source in range(blocks):
                total = came[source * harm_devices, local]
                for harm in range(1, harm_devices):
                    total = total + came[source * harm_devices + harm, local]
                for slot in range(slots):
                    amount = (source - slot) * width % LANES
                    moved = pltpu.roll(total, amount, axis=1) if amount else total
                    packed[slot] = jnp.where(lane_block == source, moved, packed[slot])
            for slot in range(slots):
                for part in range(2):
                    for at, field in enumerate(fields):
                        start = (part * count + at) * own_cells
                        target = (part * all_fields + field) * own_cells
                        out_ref[local * slots + slot, target : target + own_cells, :] = packed[
                            slot
                        ][start : start + own_cells, :]


def smem(count):
    return [pl.BlockSpec(memory_space=pltpu.SMEM)] * count


def vmem(count):
    return [pl.BlockSpec(memory_space=pltpu.VMEM)] * count


def exchanged(value, axes):
    return lax.all_to_all(value, axes, split_axis=0, concat_axis=0, tiled=True)


def body(direct_field, adjoint_field, triad_slots):
    blocks, harm_devices = lax.axis_size("mode"), lax.axis_size("harm")
    harms, slots, parts, fields, cells, radial = direct_field.shape
    width = radial // blocks
    groups, group_rows = slots * parts, fields * cells
    tile = groups * cells
    params = pltpu.CompilerParams(vmem_limit_bytes=VMEM_LIMIT)
    rad = lax.axis_index("rad").astype(jnp.int32).reshape(1)

    direct = direct_field.reshape(harms, groups, group_rows, radial)
    adjoint = adjoint_field.reshape(harms, groups, group_rows, radial)
    swap = [(0, 1), (1, 0)]
    far_direct = lax.ppermute(direct, "rad", swap)
    far_adjoint = lax.ppermute(adjoint, "rad", swap)

    def payload(rows):
        return jax.ShapeDtypeStruct((blocks, rows, LANES), jnp.bfloat16)

    sizes = (harms, blocks, width)
    main_matrix = pltpu.VMEM((harms * LANES, blocks * LANES), jnp.bfloat16)
    lead = pl.pallas_call(
        functools.partial(first_pack_kernel, sizes, cells),
        out_shape=payload(2 * len(GROUPS[0]) * tile + 2 * group_rows + SLOT_ROWS),
        in_specs=smem(2) + vmem(4),
        out_specs=vmem(1)[0],
        scratch_shapes=[
            main_matrix,
            pltpu.VMEM((2 * harms * LANES, blocks * LANES), jnp.bfloat16),
        ],
        compiler_params=params,
        name="pack_first",
    )(rad, triad_slots.reshape(-1), direct, adjoint, far_direct, far_adjoint)
    came = [exchanged(lead, "mode")]
    if len(GROUPS) > 1:
        shapes = [payload(2 * len(group) * tile) for group in GROUPS[1:]]
        rest = pl.pallas_call(
            functools.partial(rest_pack_kernel, sizes, cells),
            out_shape=shapes,
            in_specs=vmem(2),
            out_specs=vmem(len(shapes)),
            scratch_shapes=[main_matrix],
            compiler_params=params,
            name="pack_rest",
        )(direct, adjoint)
        came += [exchanged(value, "mode") for value in rest]

    per_harm, own_cells = blocks // harm_devices, cells // blocks
    sizes = (harms, blocks, width, groups, slots, fields, cells, harm_devices)
    listed = (max(blocks, 8), LANES)
    owned = []
    for index, group in enumerate(GROUPS):
        count = len(group)
        operands = [came[0]] + ([came[index]] if index else [])
        derived = pltpu.VMEM((2 * count, blocks * groups, cells, LANES), jnp.float32)
        sent = pl.pallas_call(
            functools.partial(triad_kernel, sizes, group),
            out_shape=jax.ShapeDtypeStruct(
                (blocks * harm_devices, per_harm, 2 * count * own_cells, LANES), jnp.float32
            ),
            in_specs=vmem(len(operands)),
            out_specs=vmem(1)[0],
            scratch_shapes=[
                pltpu.VMEM((groups, 2 * LANES, LANES), jnp.bfloat16),
                pltpu.VMEM((tile, tile), jnp.bfloat16),
                pltpu.VMEM((4, blocks * groups, cells, LANES), jnp.float32),
                derived,
                derived,
                pltpu.VMEM((blocks * slots, 2 * count, cells, LANES), jnp.float32),
                pltpu.VMEM(listed, jnp.int32),
                pltpu.SMEM(listed, jnp.int32),
                pltpu.SemaphoreType.DMA,
            ],
            compiler_params=params,
            name="triads",
        )(*operands)
        owned.append(exchanged(sent, ("mode", "harm")))

    sizes = (blocks, harm_devices, slots, width, per_harm, own_cells, fields)
    result = pl.pallas_call(
        functools.partial(unpack_kernel, sizes),
        out_shape=jax.ShapeDtypeStruct(
            (per_harm * slots, 2 * fields * own_cells, LANES), jnp.float32
        ),
        in_specs=vmem(len(owned)),
        out_specs=vmem(1)[0],
        compiler_params=params,
        name="unpack",
    )(*owned)
    return result.reshape(per_harm * slots, 2, fields, own_cells, radial)


def solution(mesh):
    return jax.shard_map(
        body,
        mesh=mesh,
        in_specs=(
            P(("case", "harm"), "mode", None, None, None, "rad"),
            P(("case", "harm"), "mode", None, None, None, "rad"),
            P("mode", None, None),
        ),
        out_specs=P(("case", "harm"), None, None, "mode", "rad"),
        check_vma=False,
    )
```

```python
import functools
import math

import jax
import jax.numpy as jnp
from jax import lax
from jax.experimental import pallas as pl
from jax.experimental.pallas import tpu as pltpu
from jax.sharding import PartitionSpec as P

HARMS = 8
LANES = 128
HALO = 4
SLOT_ROWS = 16
GROUPS = ((1, 2), (0, 3, 4))
VMEM_LIMIT = 40 * 1024 * 1024


def iota(shape, axis):
    return lax.broadcasted_iota(jnp.int32, shape, axis)


def one_hot(mask):
    return jnp.where(mask, 1.0, 0.0).astype(jnp.bfloat16)


def halo_offset(index, width):
    return jnp.where(index < 2, index - 2, index - 2 + width)


def wrapped(index, count):
    return jnp.where(index >= count, index - count, index)


def columns(harms, blocks):
    shape = (harms * LANES, blocks * LANES)
    row, col = iota(shape, 0), iota(shape, 1)
    return row // LANES, row % LANES, col // LANES, col % LANES


def side_by_side(ref, group, rows):
    return jnp.concatenate([ref[k, group, rows, :] for k in range(ref.shape[0])], axis=1)


def fill_main(matrix, sizes):
    harms, blocks, width = sizes
    harm_in, cell_in, owner, lane = columns(harms, blocks)
    matrix[...] = one_hot(
        (lane // width == harm_in) & (cell_in == owner * width + lane % width)
    )


def main_pack_kernel(sizes, pieces, *refs):
    ins, out, matrix = refs[:pieces], refs[-2], refs[-1]
    fill_main(matrix, sizes)
    groups, cells = ins[0].shape[1], ins[0].shape[2]
    rows = [side_by_side(ref, group, slice(0, cells)) for ref in ins for group in range(groups)]
    main = jnp.dot(jnp.concatenate(rows, axis=0), matrix[...], preferred_element_type=jnp.float32)
    for owner in range(out.shape[0]):
        out[owner, 0 : main.shape[0], :] = main[:, owner * LANES : (owner + 1) * LANES].astype(
            jnp.bfloat16
        )


def halo_pack_kernel(
    sizes, base, rad, slots, d_hbm, a_hbm, far_d, far_a, _, out, own_d, own_a, halo_m, ends_v, sems
):
    harms, blocks, width = sizes
    groups, group_rows = own_d.shape[1], own_d.shape[2]
    loads = []
    for array, (source, target) in enumerate(((d_hbm, own_d), (a_hbm, own_a))):
        for k in range(harms):
            loads.append(pltpu.make_async_copy(source.at[k], target.at[k], sems.at[array, k]))
    for load in loads:
        load.start()
    shift = jnp.where(rad[0] == 0, LANES, -LANES)
    depth = harms * LANES
    span_h = harms * HALO
    harm_in, cell_in, owner, lane = columns(harms, blocks)
    part = lane % span_h
    wanted = owner * width + halo_offset(part % HALO, width)
    same = (part // HALO == harm_in) & (lane < groups * span_h)
    halo_m[0:depth, :] = one_hot(same & (cell_in == wanted))
    halo_m[depth:, :] = one_hot(same & (cell_in + shift == wanted))
    lane_group = (iota((group_rows, blocks * LANES), 1) % LANES) // span_h
    everything = slice(0, group_rows)
    for load in loads:
        load.wait()
    for array, (own, far) in enumerate(((own_d, far_d), (own_a, far_a))):
        pieces = [
            jnp.concatenate(
                [side_by_side(own, group, everything), side_by_side(far, group, everything)], axis=1
            )
            for group in range(groups)
        ]
        ends = jnp.dot(
            jnp.concatenate(pieces, axis=0), halo_m[...], preferred_element_type=jnp.float32
        )
        held = jnp.zeros((group_rows, blocks * LANES), jnp.float32)
        for group in range(groups):
            held = jnp.where(
                lane_group == group, ends[group * group_rows : (group + 1) * group_rows], held
            )
        start = array * group_rows
        for block in range(blocks):
            ends_v[block, start : start + group_rows, :] = held[
                :, block * LANES : (block + 1) * LANES
            ].astype(jnp.bfloat16)
    lane = iota((SLOT_ROWS, LANES), 1)
    listed = jnp.zeros((SLOT_ROWS, LANES), jnp.int32)
    for index in range(slots.shape[0]):
        listed = jnp.where(lane == index, slots[index], listed)
    start = 2 * group_rows
    for block in range(blocks):
        ends_v[block, start:, :] = listed.astype(jnp.float32).astype(jnp.bfloat16)
    store = pltpu.make_async_copy(
        ends_v, out.at[:, base : base + start + SLOT_ROWS, :], sems.at[0, harms]
    )
    store.start()
    store.wait()


def coefficient(distance):
    near = jnp.where(distance == 1, 8.0, jnp.where(distance == -1, -8.0, 0.0))
    return jnp.where(distance == 2, -1.0, jnp.where(distance == -2, 1.0, near))


def triad_kernel(sizes, fields, *refs):
    harms, blocks, width, groups, slots, all_fields, cells, harm_devices = sizes
    first = fields == GROUPS[0]
    lead, main = refs[0], refs[0 if first else 1]
    at = 1 if first else 2
    out, radial_m, axial_m, plain_v, axial_v, radial_v, sums, slots_v, slots_s, slots_sem = refs[at:]
    halo_row = 2 * len(GROUPS[0]) * groups * cells
    slot_row = halo_row + 2 * all_fields * cells
    for block in range(blocks):
        slots_v[block : block + 1, :] = (
            lead[block, slot_row : slot_row + SLOT_ROWS, :].astype(jnp.float32)[0:1, :]
        ).astype(jnp.int32)
    listing = pltpu.make_async_copy(slots_v, slots_s, slots_sem)
    listing.start()
    count = len(fields)
    span_h = harms * HALO
    used = harms * width
    tile = groups * cells
    shape = (LANES, LANES)
    row, col = iota(shape, 0), iota(shape, 1)
    inside = (row // width == col // width) & (row < used) & (col < used)
    within = jnp.where(inside, coefficient(row - col), 0.0).astype(jnp.bfloat16)
    square = (tile, tile)
    row_t, col_t = iota(square, 0), iota(square, 1)
    axial_m[...] = jnp.where(
        row_t // cells == col_t // cells, coefficient(col_t - row_t), 0.0
    ).astype(jnp.bfloat16)

    for group in range(groups):
        part = row - group * span_h
        mine = (part >= 0) & (part < span_h) & (col < used) & (part // HALO == col // width)
        place = halo_offset(part % HALO, width)
        around = jnp.where(mine, coefficient(place - col % width), 0.0).astype(jnp.bfloat16)
        radial_m[group] = jnp.concatenate([within, around], axis=0)
    for group in range(groups):
        pieces = []
        for array in range(2):
            for local, field in enumerate(fields):
                for step in range(blocks):
                    start = ((array * count + local) * groups + group) * cells
                    beside = halo_row + (array * all_fields + field) * cells
                    pieces.append(
                        jnp.concatenate(
                            [
                                main[step, start : start + cells, :],
                                lead[step, beside : beside + cells, :],
                            ],
                            axis=1,
                        )
                    )
        slopes = jnp.dot(
            jnp.concatenate(pieces, axis=0), radial_m[group], preferred_element_type=jnp.float32
        )
        index = 0
        for array in range(2):
            for local in range(count):
                for step in range(blocks):
                    radial_v[array * count + local, step * groups + group] = slopes[
                        index * cells : (index + 1) * cells, :
                    ]
                    index += 1
    for step in range(blocks):
        for local in range(count):
            starts = [(array * count + local) * tile for array in range(2)]
            both = jnp.concatenate([main[step, s : s + tile, :] for s in starts], axis=1)
            slopes = jnp.dot(axial_m[...], both, preferred_element_type=jnp.float32)
            for array in range(2):
                for group in range(groups):
                    axial_v[array * count + local, step * groups + group] = slopes[
                        group * cells : (group + 1) * cells, array * LANES : (array + 1) * LANES
                    ]
        for which in range(4):
            for group in range(groups):
                held = which // 2 * len(GROUPS[0]) + which % 2
                start = (held * groups + group) * cells
                plain_v[which, step * groups + group] = lead[
                    step, start : start + cells, :
                ].astype(jnp.float32)

    listing.wait()

    @pl.loop(0, blocks * slots)
    def _(index):
        step = index // slots
        entry = lax.rem(index, slots) * blocks

        def add_stop(stop, running):
            source = wrapped(step - stop + blocks, blocks)
            at_a = step * groups + slots_s[step, (entry + stop) * 2] * 2
            at_d = source * groups + slots_s[step, (entry + stop) * 2 + 1] * 2
            d1r, d1i, d2r, d2i = (plain_v[w, at_d + c] for w in (0, 1) for c in (0, 1))
            a1r, a1i, a2r, a2i = (plain_v[w, at_a + c] for w in (2, 3) for c in (0, 1))
            result = []
            for local in range(count):
                xar, xai = axial_v[count + local, at_a], axial_v[count + local, at_a + 1]
                rar, rai = radial_v[count + local, at_a], radial_v[count + local, at_a + 1]
                xdr, xdi = axial_v[local, at_d], axial_v[local, at_d + 1]
                rdr, rdi = radial_v[local, at_d], radial_v[local, at_d + 1]
                real = (d1r * xar + d1i * xai) + (d2r * rar + d2i * rai)
                real = real + ((xdr * a1r + xdi * a1i) + (rdr * a2r + rdi * a2i))
                imag = (d1r * xai - d1i * xar) + (d2r * rai - d2i * rar)
                imag = imag + ((xdr * a1i - xdi * a1r) + (rdr * a2i - rdi * a2r))
                old_real, old_imag = running[local]
                result.append((old_real + real, old_imag + imag))
            return tuple(result)

        zero = jnp.zeros((cells, LANES), jnp.float32)
        running = tuple((zero, zero) for _ in range(count))
        if blocks <= 4:
            for stop in range(blocks):
                running = add_stop(stop, running)
        else:
            running = lax.fori_loop(0, blocks, add_stop, running)
        for local in range(count):
            for part in range(2):
                sums[index, part * count + local] = running[local][part]

    scale = 1.0 / (12.0 * math.sqrt(8.0 * blocks * HARMS))
    per_harm = blocks // harm_devices
    own_cells = cells // blocks
    lane_slot = iota((cells, LANES), 1) // width

    @pl.loop(0, blocks)
    def _(step):
        for row in range(2 * count):
            packed = jnp.zeros((cells, LANES), jnp.float32)
            for slot in range(slots):
                value = sums[step * slots + slot, row]
                reach = harms // 2
                while reach:
                    value = value + pltpu.roll(value, reach * width, axis=1)
                    reach //= 2
                if used < LANES and slot:
                    value = pltpu.roll(value, slot * width, axis=1)
                packed = jnp.where(lane_slot == slot, value, packed)
            packed = packed * scale
            for owner in range(blocks):
                out[
                    owner * harm_devices + step // per_harm,
                    lax.rem(step, per_harm),
                    row * own_cells : (row + 1) * own_cells,
                    :,
                ] = packed[owner * own_cells : (owner + 1) * own_cells, :]


def unpack_kernel(sizes, *refs):
    blocks, harm_devices, slots, width, per_harm, own_cells, all_fields = sizes
    ins, out_ref = refs[:-1], refs[-1]
    for came, fields in zip(ins, GROUPS):
        count = len(fields)
        rows = 2 * count * own_cells
        lane_block = iota((rows, LANES), 1) // width
        for local in range(per_harm):
            packed = [jnp.zeros((rows, LANES), jnp.float32) for _ in range(slots)]
            for source in range(blocks):
                total = came[source * harm_devices, local]
                for harm in range(1, harm_devices):
                    total = total + came[source * harm_devices + harm, local]
                for slot in range(slots):
                    amount = (source - slot) * width % LANES
                    moved = pltpu.roll(total, amount, axis=1) if amount else total
                    packed[slot] = jnp.where(lane_block == source, moved, packed[slot])
            for slot in range(slots):
                for part in range(2):
                    for at, field in enumerate(fields):
                        start = (part * count + at) * own_cells
                        target = (part * all_fields + field) * own_cells
                        out_ref[local * slots + slot, target : target + own_cells, :] = packed[
                            slot
                        ][start : start + own_cells, :]


def smem(count):
    return [pl.BlockSpec(memory_space=pltpu.SMEM)] * count


def vmem(count):
    return [pl.BlockSpec(memory_space=pltpu.VMEM)] * count


def anywhere(count):
    return [pl.BlockSpec(memory_space=pl.ANY)] * count


def exchanged(value, axes):
    return lax.all_to_all(value, axes, split_axis=0, concat_axis=0, tiled=True)


def body(direct_field, adjoint_field, triad_slots):
    blocks, harm_devices = lax.axis_size("mode"), lax.axis_size("harm")
    harms, slots, parts, fields, cells, radial = direct_field.shape
    width = radial // blocks
    groups, group_rows = slots * parts, fields * cells
    tile = groups * cells
    params = pltpu.CompilerParams(vmem_limit_bytes=VMEM_LIMIT)
    rad = lax.axis_index("rad").astype(jnp.int32).reshape(1)

    direct = direct_field.reshape(harms, groups, group_rows, radial)
    adjoint = adjoint_field.reshape(harms, groups, group_rows, radial)
    swap = [(0, 1), (1, 0)]
    far_direct = lax.ppermute(direct, "rad", swap)
    far_adjoint = lax.ppermute(adjoint, "rad", swap)

    def payload(rows):
        return jax.ShapeDtypeStruct((blocks, rows, LANES), jnp.bfloat16)

    sizes = (harms, blocks, width)
    tail = 2 * group_rows + SLOT_ROWS

    def packed(group, extra, after):
        ins = [direct] * len(group) + [adjoint] * len(group)
        return pl.pallas_call(
            functools.partial(main_pack_kernel, sizes, len(ins)),
            grid=(1,),
            out_shape=payload(len(ins) * tile + extra),
            in_specs=[
                pl.BlockSpec((harms, groups, cells, radial), lambda i, f=field: (0, 0, f, 0))
                for field in group + group
            ]
            + anywhere(len(after)),
            out_specs=vmem(1)[0],
            scratch_shapes=[pltpu.VMEM((harms * LANES, blocks * LANES), jnp.bfloat16)],
            compiler_params=params,
            name="pack_main",
        )(*ins, *after)

    lead = packed(GROUPS[0], tail, [])
    lead = pl.pallas_call(
        functools.partial(halo_pack_kernel, sizes, 2 * len(GROUPS[0]) * tile),
        out_shape=jax.ShapeDtypeStruct(lead.shape, lead.dtype),
        in_specs=smem(2) + anywhere(2) + vmem(2) + anywhere(1),
        out_specs=anywhere(1)[0],
        scratch_shapes=[
            pltpu.VMEM(direct.shape, jnp.bfloat16),
            pltpu.VMEM(adjoint.shape, jnp.bfloat16),
            pltpu.VMEM((2 * harms * LANES, blocks * LANES), jnp.bfloat16),
            pltpu.VMEM((blocks, tail, LANES), jnp.bfloat16),
            pltpu.SemaphoreType.DMA((2, harms + 1)),
        ],
        input_output_aliases={6: 0},
        compiler_params=params,
        name="pack_halos",
    )(rad, triad_slots.reshape(-1), direct, adjoint, far_direct, far_adjoint, lead)
    came = [exchanged(lead, "mode")]
    last = lead
    for group in GROUPS[1:]:
        last = packed(group, 0, [last])
        came.append(exchanged(last, "mode"))

    per_harm, own_cells = blocks // harm_devices, cells // blocks
    sizes = (harms, blocks, width, groups, slots, fields, cells, harm_devices)
    listed = (max(blocks, 8), LANES)
    owned = []
    for index, group in enumerate(GROUPS):
        count = len(group)
        operands = [came[0]] + ([came[index]] if index else [])
        derived = pltpu.VMEM((2 * count, blocks * groups, cells, LANES), jnp.float32)
        sent = pl.pallas_call(
            functools.partial(triad_kernel, sizes, group),
            out_shape=jax.ShapeDtypeStruct(
                (blocks * harm_devices, per_harm, 2 * count * own_cells, LANES), jnp.float32
            ),
            in_specs=vmem(len(operands)),
            out_specs=vmem(1)[0],
            scratch_shapes=[
                pltpu.VMEM((groups, 2 * LANES, LANES), jnp.bfloat16),
                pltpu.VMEM((tile, tile), jnp.bfloat16),
                pltpu.VMEM((4, blocks * groups, cells, LANES), jnp.float32),
                derived,
                derived,
                pltpu.VMEM((blocks * slots, 2 * count, cells, LANES), jnp.float32),
                pltpu.VMEM(listed, jnp.int32),
                pltpu.SMEM(listed, jnp.int32),
                pltpu.SemaphoreType.DMA,
            ],
            compiler_params=params,
            name="triads",
        )(*operands)
        owned.append(exchanged(sent, ("mode", "harm")))

    sizes = (blocks, harm_devices, slots, width, per_harm, own_cells, fields)
    result = pl.pallas_call(
        functools.partial(unpack_kernel, sizes),
        out_shape=jax.ShapeDtypeStruct(
            (per_harm * slots, 2 * fields * own_cells, LANES), jnp.float32
        ),
        in_specs=vmem(len(owned)),
        out_specs=vmem(1)[0],
        compiler_params=params,
        name="unpack",
    )(*owned)
    return result.reshape(per_harm * slots, 2, fields, own_cells, radial)


def solution(mesh):
    return jax.shard_map(
        body,
        mesh=mesh,
        in_specs=(
            P(("case", "harm"), "mode", None, None, None, "rad"),
            P(("case", "harm"), "mode", None, None, None, "rad"),
            P("mode", None, None),
        ),
        out_specs=P(("case", "harm"), None, None, "mode", "rad"),
        check_vma=False,
    )
```

```python
import functools
import math

import jax
import jax.numpy as jnp
from jax import lax
from jax.experimental import pallas as pl
from jax.experimental.pallas import tpu as pltpu
from jax.sharding import PartitionSpec as P

HARMS = 8
LANES = 128
HALO = 4
SLOT_ROWS = 16
GROUPS = ((1, 2), (0, 3, 4))
VMEM_LIMIT = 40 * 1024 * 1024


def iota(shape, axis):
    return lax.broadcasted_iota(jnp.int32, shape, axis)


def one_hot(mask):
    return jnp.where(mask, 1.0, 0.0).astype(jnp.bfloat16)


def halo_offset(index, width):
    return jnp.where(index < 2, index - 2, index - 2 + width)


def wrapped(index, count):
    return jnp.where(index >= count, index - count, index)


def columns(harms, blocks, first):
    shape = (harms * LANES, blocks * LANES)
    row, col = iota(shape, 0), iota(shape, 1)
    owner = wrapped(col // LANES + first, blocks)
    return row // LANES, row % LANES, owner, col % LANES


def side_by_side(ref, group, rows):
    return jnp.concatenate([ref[k, group, rows, :] for k in range(ref.shape[0])], axis=1)


def fill_main(matrix, sizes, first):
    harms, blocks, width = sizes
    harm_in, cell_in, owner, lane = columns(harms, blocks, first)
    matrix[...] = one_hot(
        (lane // width == harm_in) & (cell_in == owner * width + lane % width)
    )


def main_slabs(sizes, fields, first, own_d, own_a, matrix, cells):
    fill_main(matrix, sizes, first)
    rows = []
    for ref in (own_d, own_a):
        for field in fields:
            piece = slice(field * cells, (field + 1) * cells)
            rows += [side_by_side(ref, group, piece) for group in range(ref.shape[1])]
    main = jnp.dot(jnp.concatenate(rows, axis=0), matrix[...], preferred_element_type=jnp.float32)
    main = main.astype(jnp.bfloat16)
    return [main[:, owner * LANES : (owner + 1) * LANES] for owner in range(sizes[1])]


def lead_pack_kernel(sizes, cells, own_d, own_a, out, matrix):
    slabs = main_slabs(sizes, GROUPS[0], 0, own_d, own_a, matrix, cells)
    for owner, slab in enumerate(slabs):
        out[owner] = slab


def group_pack_kernel(sizes, cells, fields, mode, own_d, own_a, _, *refs):
    slabs = main_slabs(sizes, fields, mode[0], own_d, own_a, refs[-1], cells)
    for out, slab in zip(refs[:-1], slabs):
        out[...] = slab


def halo_pack_kernel(sizes, base, rad, slots, own_d, own_a, far_d, far_a, lead, out, halo_m):
    harms, blocks, width = sizes
    groups, group_rows = own_d.shape[1], own_d.shape[2]
    out[:, 0:base, :] = lead[...]
    shift = jnp.where(rad[0] == 0, LANES, -LANES)
    depth = harms * LANES
    span_h = harms * HALO
    harm_in, cell_in, owner, lane = columns(harms, blocks, 0)
    part = lane % span_h
    wanted = owner * width + halo_offset(part % HALO, width)
    same = (part // HALO == harm_in) & (lane < groups * span_h)
    halo_m[0:depth, :] = one_hot(same & (cell_in == wanted))
    halo_m[depth:, :] = one_hot(same & (cell_in + shift == wanted))
    lane_group = (iota((group_rows, blocks * LANES), 1) % LANES) // span_h
    everything = slice(0, group_rows)
    for array, (own, far) in enumerate(((own_d, far_d), (own_a, far_a))):
        pieces = [
            jnp.concatenate(
                [side_by_side(own, group, everything), side_by_side(far, group, everything)], axis=1
            )
            for group in range(groups)
        ]
        ends = jnp.dot(
            jnp.concatenate(pieces, axis=0), halo_m[...], preferred_element_type=jnp.float32
        )
        held = jnp.zeros((group_rows, blocks * LANES), jnp.float32)
        for group in range(groups):
            held = jnp.where(
                lane_group == group, ends[group * group_rows : (group + 1) * group_rows], held
            )
        start = base + array * group_rows
        for block in range(blocks):
            out[block, start : start + group_rows, :] = held[
                :, block * LANES : (block + 1) * LANES
            ].astype(jnp.bfloat16)
    lane = iota((SLOT_ROWS, LANES), 1)
    listed = jnp.zeros((SLOT_ROWS, LANES), jnp.int32)
    for index in range(slots.shape[0]):
        listed = jnp.where(lane == index, slots[index], listed)
    start = base + 2 * group_rows
    for block in range(blocks):
        out[block, start : start + SLOT_ROWS, :] = listed.astype(jnp.float32).astype(jnp.bfloat16)


def coefficient(distance):
    near = jnp.where(distance == 1, 8.0, jnp.where(distance == -1, -8.0, 0.0))
    return jnp.where(distance == 2, -1.0, jnp.where(distance == -2, 1.0, near))


def triad_kernel(sizes, fields, *refs):
    harms, blocks, width, groups, slots, all_fields, cells, harm_devices = sizes
    first = fields == GROUPS[0]
    mode, lead = refs[:2]
    mains = [lead.at[block] for block in range(blocks)] if first else refs[2 : 2 + blocks]
    origins = [step if first else wrapped(mode[0] - step + blocks, blocks) for step in range(blocks)]
    at = 2 if first else 2 + blocks
    out, radial_m, axial_m, plain_v, axial_v, radial_v, sums, slots_v, slots_s, slots_sem = refs[at:]
    halo_row = 2 * len(GROUPS[0]) * groups * cells
    slot_row = halo_row + 2 * all_fields * cells
    for block in range(blocks):
        slots_v[block : block + 1, :] = (
            lead[block, slot_row : slot_row + SLOT_ROWS, :].astype(jnp.float32)[0:1, :]
        ).astype(jnp.int32)
    listing = pltpu.make_async_copy(slots_v, slots_s, slots_sem)
    listing.start()
    count = len(fields)
    span_h = harms * HALO
    used = harms * width
    tile = groups * cells
    shape = (LANES, LANES)
    row, col = iota(shape, 0), iota(shape, 1)
    inside = (row // width == col // width) & (row < used) & (col < used)
    within = jnp.where(inside, coefficient(row - col), 0.0).astype(jnp.bfloat16)
    square = (tile, tile)
    row_t, col_t = iota(square, 0), iota(square, 1)
    axial_m[...] = jnp.where(
        row_t // cells == col_t // cells, coefficient(col_t - row_t), 0.0
    ).astype(jnp.bfloat16)

    for group in range(groups):
        part = row - group * span_h
        mine = (part >= 0) & (part < span_h) & (col < used) & (part // HALO == col // width)
        place = halo_offset(part % HALO, width)
        around = jnp.where(mine, coefficient(place - col % width), 0.0).astype(jnp.bfloat16)
        radial_m[group] = jnp.concatenate([within, around], axis=0)
    for group in range(groups):
        pieces = []
        for array in range(2):
            for local, field in enumerate(fields):
                for step in range(blocks):
                    start = ((array * count + local) * groups + group) * cells
                    beside = halo_row + (array * all_fields + field) * cells
                    pieces.append(
                        jnp.concatenate(
                            [
                                mains[step][start : start + cells, :],
                                lead[origins[step], beside : beside + cells, :],
                            ],
                            axis=1,
                        )
                    )
        slopes = jnp.dot(
            jnp.concatenate(pieces, axis=0), radial_m[group], preferred_element_type=jnp.float32
        )
        index = 0
        for array in range(2):
            for local in range(count):
                for step in range(blocks):
                    radial_v[array * count + local, origins[step] * groups + group] = slopes[
                        index * cells : (index + 1) * cells, :
                    ]
                    index += 1
    for step in range(blocks):
        for local in range(count):
            starts = [(array * count + local) * tile for array in range(2)]
            both = jnp.concatenate([mains[step][s : s + tile, :] for s in starts], axis=1)
            slopes = jnp.dot(axial_m[...], both, preferred_element_type=jnp.float32)
            for array in range(2):
                for group in range(groups):
                    axial_v[array * count + local, origins[step] * groups + group] = slopes[
                        group * cells : (group + 1) * cells, array * LANES : (array + 1) * LANES
                    ]
        for which in range(4):
            for group in range(groups):
                held = which // 2 * len(GROUPS[0]) + which % 2
                start = (held * groups + group) * cells
                plain_v[which, step * groups + group] = lead[
                    step, start : start + cells, :
                ].astype(jnp.float32)

    listing.wait()

    @pl.loop(0, blocks * slots)
    def _(index):
        step = index // slots
        entry = lax.rem(index, slots) * blocks

        def add_stop(stop, running):
            source = wrapped(step - stop + blocks, blocks)
            at_a = step * groups + slots_s[step, (entry + stop) * 2] * 2
            at_d = source * groups + slots_s[step, (entry + stop) * 2 + 1] * 2
            d1r, d1i, d2r, d2i = (plain_v[w, at_d + c] for w in (0, 1) for c in (0, 1))
            a1r, a1i, a2r, a2i = (plain_v[w, at_a + c] for w in (2, 3) for c in (0, 1))
            result = []
            for local in range(count):
                xar, xai = axial_v[count + local, at_a], axial_v[count + local, at_a + 1]
                rar, rai = radial_v[count + local, at_a], radial_v[count + local, at_a + 1]
                xdr, xdi = axial_v[local, at_d], axial_v[local, at_d + 1]
                rdr, rdi = radial_v[local, at_d], radial_v[local, at_d + 1]
                real = (d1r * xar + d1i * xai) + (d2r * rar + d2i * rai)
                real = real + ((xdr * a1r + xdi * a1i) + (rdr * a2r + rdi * a2i))
                imag = (d1r * xai - d1i * xar) + (d2r * rai - d2i * rar)
                imag = imag + ((xdr * a1i - xdi * a1r) + (rdr * a2i - rdi * a2r))
                old_real, old_imag = running[local]
                result.append((old_real + real, old_imag + imag))
            return tuple(result)

        zero = jnp.zeros((cells, LANES), jnp.float32)
        running = tuple((zero, zero) for _ in range(count))
        if blocks <= 4:
            for stop in range(blocks):
                running = add_stop(stop, running)
        else:
            running = lax.fori_loop(0, blocks, add_stop, running)
        for local in range(count):
            for part in range(2):
                sums[index, part * count + local] = running[local][part]

    scale = 1.0 / (12.0 * math.sqrt(8.0 * blocks * HARMS))
    per_harm = blocks // harm_devices
    own_cells = cells // blocks
    lane_slot = iota((cells, LANES), 1) // width

    @pl.loop(0, blocks)
    def _(step):
        for row in range(2 * count):
            packed = jnp.zeros((cells, LANES), jnp.float32)
            for slot in range(slots):
                value = sums[step * slots + slot, row]
                reach = harms // 2
                while reach:
                    value = value + pltpu.roll(value, reach * width, axis=1)
                    reach //= 2
                if used < LANES and slot:
                    value = pltpu.roll(value, slot * width, axis=1)
                packed = jnp.where(lane_slot == slot, value, packed)
            packed = packed * scale
            for owner in range(blocks):
                out[
                    owner * harm_devices + step // per_harm,
                    lax.rem(step, per_harm),
                    row * own_cells : (row + 1) * own_cells,
                    :,
                ] = packed[owner * own_cells : (owner + 1) * own_cells, :]


def unpack_kernel(sizes, *refs):
    blocks, harm_devices, slots, width, per_harm, own_cells, all_fields = sizes
    ins, out_ref = refs[:-1], refs[-1]
    for came, fields in zip(ins, GROUPS):
        count = len(fields)
        rows = 2 * count * own_cells
        lane_block = iota((rows, LANES), 1) // width
        for local in range(per_harm):
            packed = [jnp.zeros((rows, LANES), jnp.float32) for _ in range(slots)]
            for source in range(blocks):
                total = came[source * harm_devices, local]
                for harm in range(1, harm_devices):
                    total = total + came[source * harm_devices + harm, local]
                for slot in range(slots):
                    amount = (source - slot) * width % LANES
                    moved = pltpu.roll(total, amount, axis=1) if amount else total
                    packed[slot] = jnp.where(lane_block == source, moved, packed[slot])
            for slot in range(slots):
                for part in range(2):
                    for at, field in enumerate(fields):
                        start = (part * count + at) * own_cells
                        target = (part * all_fields + field) * own_cells
                        out_ref[local * slots + slot, target : target + own_cells, :] = packed[
                            slot
                        ][start : start + own_cells, :]


def smem(count):
    return [pl.BlockSpec(memory_space=pltpu.SMEM)] * count


def vmem(count):
    return [pl.BlockSpec(memory_space=pltpu.VMEM)] * count


def anywhere(count):
    return [pl.BlockSpec(memory_space=pl.ANY)] * count


def moved_up(values, axis):
    count = lax.axis_size(axis)
    result = [values[0]]
    for step in range(1, count):
        pairs = [(source, (source + step) % count) for source in range(count)]
        result.append(lax.ppermute(values[step], axis, pairs))
    return result


def exchanged(value, axes):
    return lax.all_to_all(value, axes, split_axis=0, concat_axis=0, tiled=True)


def body(direct_field, adjoint_field, triad_slots):
    blocks, harm_devices = lax.axis_size("mode"), lax.axis_size("harm")
    harms, slots, parts, fields, cells, radial = direct_field.shape
    width = radial // blocks
    groups, group_rows = slots * parts, fields * cells
    tile = groups * cells
    params = pltpu.CompilerParams(vmem_limit_bytes=VMEM_LIMIT)
    mode, rad = (lax.axis_index(axis).astype(jnp.int32).reshape(1) for axis in ("mode", "rad"))

    direct = direct_field.reshape(harms, groups, group_rows, radial)
    adjoint = adjoint_field.reshape(harms, groups, group_rows, radial)
    swap = [(0, 1), (1, 0)]
    far_direct = lax.ppermute(direct, "rad", swap)
    far_adjoint = lax.ppermute(adjoint, "rad", swap)

    sizes = (harms, blocks, width)
    tail = 2 * group_rows + SLOT_ROWS

    matrix = pltpu.VMEM((harms * LANES, blocks * LANES), jnp.bfloat16)
    base = 2 * len(GROUPS[0]) * tile
    lead = pl.pallas_call(
        functools.partial(lead_pack_kernel, sizes, cells),
        out_shape=jax.ShapeDtypeStruct((blocks, base, LANES), jnp.bfloat16),
        in_specs=vmem(2),
        out_specs=vmem(1)[0],
        scratch_shapes=[matrix],
        compiler_params=params,
        name="pack_lead",
    )(direct, adjoint)
    lead = pl.pallas_call(
        functools.partial(halo_pack_kernel, sizes, base),
        out_shape=jax.ShapeDtypeStruct((blocks, base + tail, LANES), jnp.bfloat16),
        in_specs=smem(2) + vmem(4) + vmem(1),
        out_specs=vmem(1)[0],
        scratch_shapes=[pltpu.VMEM((2 * harms * LANES, blocks * LANES), jnp.bfloat16)],
        compiler_params=params,
        name="pack_halos",
    )(rad, triad_slots.reshape(-1), direct, adjoint, far_direct, far_adjoint, lead)
    came = [[exchanged(lead, "mode")]]
    for group in GROUPS[1:]:
        slab = jax.ShapeDtypeStruct((2 * len(group) * tile, LANES), jnp.bfloat16)
        slabs = pl.pallas_call(
            functools.partial(group_pack_kernel, sizes, cells, group),
            out_shape=[slab] * blocks,
            in_specs=smem(1) + vmem(2) + anywhere(1),
            out_specs=vmem(blocks),
            scratch_shapes=[matrix],
            compiler_params=params,
            name="pack_group",
        )(mode, direct, adjoint, lead)
        came.append(moved_up(slabs, "mode"))

    per_harm, own_cells = blocks // harm_devices, cells // blocks
    sizes = (harms, blocks, width, groups, slots, fields, cells, harm_devices)
    listed = (max(blocks, 8), LANES)
    owned = []
    for index, group in enumerate(GROUPS):
        count = len(group)
        operands = came[0] + (came[index] if index else [])
        derived = pltpu.VMEM((2 * count, blocks * groups, cells, LANES), jnp.float32)
        sent = pl.pallas_call(
            functools.partial(triad_kernel, sizes, group),
            out_shape=jax.ShapeDtypeStruct(
                (blocks * harm_devices, per_harm, 2 * count * own_cells, LANES), jnp.float32
            ),
            in_specs=smem(1) + vmem(len(operands)),
            out_specs=vmem(1)[0],
            scratch_shapes=[
                pltpu.VMEM((groups, 2 * LANES, LANES), jnp.bfloat16),
                pltpu.VMEM((tile, tile), jnp.bfloat16),
                pltpu.VMEM((4, blocks * groups, cells, LANES), jnp.float32),
                derived,
                derived,
                pltpu.VMEM((blocks * slots, 2 * count, cells, LANES), jnp.float32),
                pltpu.VMEM(listed, jnp.int32),
                pltpu.SMEM(listed, jnp.int32),
                pltpu.SemaphoreType.DMA,
            ],
            compiler_params=params,
            name="triads",
        )(mode, *operands)
        owned.append(exchanged(sent, ("mode", "harm")))

    sizes = (blocks, harm_devices, slots, width, per_harm, own_cells, fields)
    result = pl.pallas_call(
        functools.partial(unpack_kernel, sizes),
        out_shape=jax.ShapeDtypeStruct(
            (per_harm * slots, 2 * fields * own_cells, LANES), jnp.float32
        ),
        in_specs=vmem(len(owned)),
        out_specs=vmem(1)[0],
        compiler_params=params,
        name="unpack",
    )(*owned)
    return result.reshape(per_harm * slots, 2, fields, own_cells, radial)


def solution(mesh):
    return jax.shard_map(
        body,
        mesh=mesh,
        in_specs=(
            P(("case", "harm"), "mode", None, None, None, "rad"),
            P(("case", "harm"), "mode", None, None, None, "rad"),
            P("mode", None, None),
        ),
        out_specs=P(("case", "harm"), None, None, "mode", "rad"),
        check_vma=False,
    )
```

```python
import functools
import math

import jax
import jax.numpy as jnp
from jax import lax
from jax.experimental import pallas as pl
from jax.experimental.pallas import tpu as pltpu
from jax.sharding import PartitionSpec as P

HARMS = 8
LANES = 128
HALO = 4
SLOT_ROWS = 16
VMEM_LIMIT = 40 * 1024 * 1024


def iota(shape, axis):
    return lax.broadcasted_iota(jnp.int32, shape, axis)


def one_hot(mask):
    return jnp.where(mask, 1.0, 0.0).astype(jnp.bfloat16)


def halo_offset(index, width):
    return jnp.where(index < 2, index - 2, index - 2 + width)


def wrapped(index, count):
    return jnp.where(index >= count, index - count, index)


def columns(harms, blocks, first):
    shape = (harms * LANES, blocks * LANES)
    row, col = iota(shape, 0), iota(shape, 1)
    owner = wrapped(col // LANES + first, blocks)
    return row // LANES, row % LANES, owner, col % LANES


def side_by_side(ref, group, rows):
    return jnp.concatenate([ref[k, group, rows, :] for k in range(ref.shape[0])], axis=1)


def matrix_kernel(sizes, groups, mode, rad, direct, adjoint, main_m, halo_m, own_d, own_a, sems):
    harms, blocks, width = sizes
    loads = [
        pltpu.make_async_copy(source.at[k], target.at[k], sems.at[array, k])
        for array, (source, target) in enumerate(((direct, own_d), (adjoint, own_a)))
        for k in range(harms)
    ]
    for load in loads:
        load.start()
    harm_in, cell_in, owner, lane = columns(harms, blocks, mode[0])
    main_m[...] = one_hot(
        (lane // width == harm_in) & (cell_in == owner * width + lane % width)
    )
    shift = jnp.where(rad[0] == 0, LANES, -LANES)
    depth = harms * LANES
    span_h = harms * HALO
    part = lane % span_h
    wanted = owner * width + halo_offset(part % HALO, width)
    same = (part // HALO == harm_in) & (lane < groups * span_h)
    halo_m[0:depth, :] = one_hot(same & (cell_in == wanted))
    halo_m[depth:, :] = one_hot(same & (cell_in + shift == wanted))
    for load in loads:
        load.wait()


def pack_kernel(sizes, cells, slots, own_d, own_a, far_d, far_a, main_m, halo_m, *outs):
    harms, blocks, width = sizes
    groups, group_rows = own_d.shape[1], own_d.shape[2]
    fields = group_rows // cells
    tile = groups * cells
    lane_group = (iota((group_rows, blocks * LANES), 1) % LANES) // (harms * HALO)
    everything = slice(0, group_rows)
    base = 2 * fields * tile
    for array, (own, far) in enumerate(((own_d, far_d), (own_a, far_a))):
        near = [side_by_side(own, group, everything) for group in range(groups)]
        rows = [
            near[group][field * cells : (field + 1) * cells, :]
            for field in range(fields)
            for group in range(groups)
        ]
        main = jnp.dot(
            jnp.concatenate(rows, axis=0), main_m[...], preferred_element_type=jnp.float32
        )
        pieces = [
            jnp.concatenate([near[group], side_by_side(far, group, everything)], axis=1)
            for group in range(groups)
        ]
        ends = jnp.dot(
            jnp.concatenate(pieces, axis=0), halo_m[...], preferred_element_type=jnp.float32
        )
        held = jnp.zeros((group_rows, blocks * LANES), jnp.float32)
        for group in range(groups):
            held = jnp.where(
                lane_group == group, ends[group * group_rows : (group + 1) * group_rows], held
            )
        for step, out in enumerate(outs):
            lanes = slice(step * LANES, (step + 1) * LANES)
            start = array * fields * tile
            out[start : start + fields * tile, :] = main[:, lanes].astype(jnp.bfloat16)
            start = base + array * group_rows
            out[start : start + group_rows, :] = held[:, lanes].astype(jnp.bfloat16)
    lane = iota((SLOT_ROWS, LANES), 1)
    listed = jnp.zeros((SLOT_ROWS, LANES), jnp.int32)
    for index in range(slots.shape[0]):
        listed = jnp.where(lane == index, slots[index], listed)
    for out in outs:
        out[base + 2 * group_rows :, :] = listed.astype(jnp.float32).astype(jnp.bfloat16)


def coefficient(distance):
    near = jnp.where(distance == 1, 8.0, jnp.where(distance == -1, -8.0, 0.0))
    return jnp.where(distance == 2, -1.0, jnp.where(distance == -2, 1.0, near))


def triad_kernel(sizes, mode, *refs):
    harms, blocks, width, groups, slots, count, cells, harm_devices = sizes
    mains = refs[:blocks]
    origins = [wrapped(mode[0] - step + blocks, blocks) for step in range(blocks)]
    out, radial_m, axial_m, plain_v, axial_v, radial_v, sums, slots_v, slots_s, slots_sem = refs[
        blocks:
    ]
    halo_row = 2 * count * groups * cells
    slot_row = halo_row + 2 * count * cells
    for step in range(blocks):
        slots_v[step : step + 1, :] = (
            mains[step][slot_row : slot_row + SLOT_ROWS, :].astype(jnp.float32)[0:1, :]
        ).astype(jnp.int32)
    listing = pltpu.make_async_copy(slots_v, slots_s, slots_sem)
    listing.start()
    span_h = harms * HALO
    used = harms * width
    tile = groups * cells
    shape = (LANES, LANES)
    row, col = iota(shape, 0), iota(shape, 1)
    inside = (row // width == col // width) & (row < used) & (col < used)
    within = jnp.where(inside, coefficient(row - col), 0.0).astype(jnp.bfloat16)
    square = (tile, tile)
    row_t, col_t = iota(square, 0), iota(square, 1)
    axial_m[...] = jnp.where(
        row_t // cells == col_t // cells, coefficient(col_t - row_t), 0.0
    ).astype(jnp.bfloat16)

    for group in range(groups):
        part = row - group * span_h
        mine = (part >= 0) & (part < span_h) & (col < used) & (part // HALO == col // width)
        place = halo_offset(part % HALO, width)
        around = jnp.where(mine, coefficient(place - col % width), 0.0).astype(jnp.bfloat16)
        radial_m[group] = jnp.concatenate([within, around], axis=0)
    for group in range(groups):
        pieces = []
        for array in range(2):
            for local in range(count):
                for step in range(blocks):
                    start = ((array * count + local) * groups + group) * cells
                    beside = halo_row + (array * count + local) * cells
                    pieces.append(
                        jnp.concatenate(
                            [
                                mains[step][start : start + cells, :],
                                mains[step][beside : beside + cells, :],
                            ],
                            axis=1,
                        )
                    )
        slopes = jnp.dot(
            jnp.concatenate(pieces, axis=0), radial_m[group], preferred_element_type=jnp.float32
        )
        index = 0
        for array in range(2):
            for local in range(count):
                for step in range(blocks):
                    radial_v[array * count + local, origins[step] * groups + group] = slopes[
                        index * cells : (index + 1) * cells, :
                    ]
                    index += 1
    for step in range(blocks):
        for local in range(count):
            starts = [(array * count + local) * tile for array in range(2)]
            both = jnp.concatenate([mains[step][s : s + tile, :] for s in starts], axis=1)
            slopes = jnp.dot(axial_m[...], both, preferred_element_type=jnp.float32)
            for array in range(2):
                for group in range(groups):
                    axial_v[array * count + local, origins[step] * groups + group] = slopes[
                        group * cells : (group + 1) * cells, array * LANES : (array + 1) * LANES
                    ]
        for which in range(4):
            for group in range(groups):
                held = which // 2 * count + 1 + which % 2
                start = (held * groups + group) * cells
                plain_v[which, origins[step] * groups + group] = mains[step][
                    start : start + cells, :
                ].astype(jnp.float32)

    listing.wait()

    @pl.loop(0, blocks * slots)
    def _(index):
        step = index // slots
        listed = wrapped(mode[0] - step + blocks, blocks)
        entry = lax.rem(index, slots) * blocks

        def add_stop(stop, running):
            source = wrapped(step - stop + blocks, blocks)
            at_a = step * groups + slots_s[listed, (entry + stop) * 2] * 2
            at_d = source * groups + slots_s[listed, (entry + stop) * 2 + 1] * 2
            d1r, d1i, d2r, d2i = (plain_v[w, at_d + c] for w in (0, 1) for c in (0, 1))
            a1r, a1i, a2r, a2i = (plain_v[w, at_a + c] for w in (2, 3) for c in (0, 1))
            result = []
            for local in range(count):
                xar, xai = axial_v[count + local, at_a], axial_v[count + local, at_a + 1]
                rar, rai = radial_v[count + local, at_a], radial_v[count + local, at_a + 1]
                xdr, xdi = axial_v[local, at_d], axial_v[local, at_d + 1]
                rdr, rdi = radial_v[local, at_d], radial_v[local, at_d + 1]
                real = (d1r * xar + d1i * xai) + (d2r * rar + d2i * rai)
                real = real + ((xdr * a1r + xdi * a1i) + (rdr * a2r + rdi * a2i))
                imag = (d1r * xai - d1i * xar) + (d2r * rai - d2i * rar)
                imag = imag + ((xdr * a1i - xdi * a1r) + (rdr * a2i - rdi * a2r))
                old_real, old_imag = running[local]
                result.append((old_real + real, old_imag + imag))
            return tuple(result)

        zero = jnp.zeros((cells, LANES), jnp.float32)
        running = tuple((zero, zero) for _ in range(count))
        if blocks <= 4:
            for stop in range(blocks):
                running = add_stop(stop, running)
        else:
            running = lax.fori_loop(0, blocks, add_stop, running)
        for local in range(count):
            for part in range(2):
                sums[index, part * count + local] = running[local][part]

    scale = 1.0 / (12.0 * math.sqrt(8.0 * blocks * HARMS))
    per_harm = blocks // harm_devices
    own_cells = cells // blocks
    lane_slot = iota((cells, LANES), 1) // width

    @pl.loop(0, blocks)
    def _(step):
        for row in range(2 * count):
            packed = jnp.zeros((cells, LANES), jnp.float32)
            for slot in range(slots):
                value = sums[step * slots + slot, row]
                reach = harms // 2
                while reach:
                    value = value + pltpu.roll(value, reach * width, axis=1)
                    reach //= 2
                if used < LANES and slot:
                    value = pltpu.roll(value, slot * width, axis=1)
                packed = jnp.where(lane_slot == slot, value, packed)
            packed = packed * scale
            for owner in range(blocks):
                out[
                    owner * harm_devices + step // per_harm,
                    lax.rem(step, per_harm),
                    row * own_cells : (row + 1) * own_cells,
                    :,
                ] = packed[owner * own_cells : (owner + 1) * own_cells, :]


def unpack_kernel(sizes, came, out_ref):
    blocks, harm_devices, slots, width, per_harm = sizes
    rows = came.shape[2]
    lane_block = iota((rows, LANES), 1) // width
    for local in range(per_harm):
        packed = [jnp.zeros((rows, LANES), jnp.float32) for _ in range(slots)]
        for source in range(blocks):
            total = came[source * harm_devices, local]
            for harm in range(1, harm_devices):
                total = total + came[source * harm_devices + harm, local]
            for slot in range(slots):
                amount = (source - slot) * width % LANES
                moved = pltpu.roll(total, amount, axis=1) if amount else total
                packed[slot] = jnp.where(lane_block == source, moved, packed[slot])
        for slot in range(slots):
            out_ref[local * slots + slot] = packed[slot]


def smem(count):
    return [pl.BlockSpec(memory_space=pltpu.SMEM)] * count


def vmem(count):
    return [pl.BlockSpec(memory_space=pltpu.VMEM)] * count


def moved_up(values, axis):
    count = lax.axis_size(axis)
    result = [values[0]]
    for step in range(1, count):
        pairs = [(source, (source + step) % count) for source in range(count)]
        result.append(lax.ppermute(values[step], axis, pairs))
    return result


def body(direct_field, adjoint_field, triad_slots):
    blocks, harm_devices = lax.axis_size("mode"), lax.axis_size("harm")
    harms, slots, parts, fields, cells, radial = direct_field.shape
    width = radial // blocks
    groups, group_rows = slots * parts, fields * cells
    tile = groups * cells
    params = pltpu.CompilerParams(vmem_limit_bytes=VMEM_LIMIT)
    mode, rad = (lax.axis_index(axis).astype(jnp.int32).reshape(1) for axis in ("mode", "rad"))

    direct = direct_field.reshape(harms, groups, group_rows, radial)
    adjoint = adjoint_field.reshape(harms, groups, group_rows, radial)
    swap = [(0, 1), (1, 0)]
    far_direct = lax.ppermute(direct, "rad", swap)
    far_adjoint = lax.ppermute(adjoint, "rad", swap)

    sizes = (harms, blocks, width)
    depth, span = harms * LANES, blocks * LANES
    main_m, halo_m, own_direct, own_adjoint = pl.pallas_call(
        functools.partial(matrix_kernel, sizes, groups),
        out_shape=[
            jax.ShapeDtypeStruct((depth, span), jnp.bfloat16),
            jax.ShapeDtypeStruct((2 * depth, span), jnp.bfloat16),
            jax.ShapeDtypeStruct(direct.shape, jnp.bfloat16),
            jax.ShapeDtypeStruct(direct.shape, jnp.bfloat16),
        ],
        in_specs=smem(2) + [pl.BlockSpec(memory_space=pl.ANY)] * 2,
        out_specs=vmem(4),
        scratch_shapes=[pltpu.SemaphoreType.DMA((2, harms))],
        compiler_params=params,
        name="matrices",
    )(mode, rad, direct, adjoint)
    payload_rows = 2 * fields * tile + 2 * group_rows + SLOT_ROWS
    slabs = pl.pallas_call(
        functools.partial(pack_kernel, sizes, cells),
        out_shape=[jax.ShapeDtypeStruct((payload_rows, LANES), jnp.bfloat16)] * blocks,
        in_specs=smem(1) + vmem(6),
        out_specs=vmem(blocks),
        compiler_params=params,
        name="pack",
    )(triad_slots.reshape(-1), own_direct, own_adjoint, far_direct, far_adjoint, main_m, halo_m)
    came = moved_up(slabs, "mode")

    per_harm, own_cells = blocks // harm_devices, cells // blocks
    sizes = (harms, blocks, width, groups, slots, fields, cells, harm_devices)
    listed = (max(blocks, 8), LANES)
    derived = pltpu.VMEM((2 * fields, blocks * groups, cells, LANES), jnp.float32)
    out_rows = 2 * fields * own_cells
    sent = pl.pallas_call(
        functools.partial(triad_kernel, sizes),
        out_shape=jax.ShapeDtypeStruct(
            (blocks * harm_devices, per_harm, out_rows, LANES), jnp.float32
        ),
        in_specs=smem(1) + vmem(blocks),
        out_specs=vmem(1)[0],
        scratch_shapes=[
            pltpu.VMEM((groups, 2 * LANES, LANES), jnp.bfloat16),
            pltpu.VMEM((tile, tile), jnp.bfloat16),
            pltpu.VMEM((4, blocks * groups, cells, LANES), jnp.float32),
            derived,
            derived,
            pltpu.VMEM((blocks * slots, 2 * fields, cells, LANES), jnp.float32),
            pltpu.VMEM(listed, jnp.int32),
            pltpu.SMEM(listed, jnp.int32),
            pltpu.SemaphoreType.DMA,
        ],
        compiler_params=params,
        name="triads",
    )(mode, *came)
    owned = lax.all_to_all(sent, ("mode", "harm"), split_axis=0, concat_axis=0, tiled=True)

    result = pl.pallas_call(
        functools.partial(unpack_kernel, (blocks, harm_devices, slots, width, per_harm)),
        out_shape=jax.ShapeDtypeStruct((per_harm * slots, out_rows, LANES), jnp.float32),
        in_specs=vmem(1),
        out_specs=vmem(1)[0],
        compiler_params=params,
        name="unpack",
    )(owned)
    return result.reshape(per_harm * slots, 2, fields, own_cells, radial)


def solution(mesh):
    return jax.shard_map(
        body,
        mesh=mesh,
        in_specs=(
            P(("case", "harm"), "mode", None, None, None, "rad"),
            P(("case", "harm"), "mode", None, None, None, "rad"),
            P("mode", None, None),
        ),
        out_specs=P(("case", "harm"), None, None, "mode", "rad"),
        check_vma=False,
    )
```

```python
import functools
import math

import jax
import jax.numpy as jnp
from jax import lax
from jax.experimental import pallas as pl
from jax.experimental.pallas import tpu as pltpu
from jax.sharding import PartitionSpec as P

HARMS = 8
LANES = 128
HALO = 4
SLOT_ROWS = 16
VMEM_LIMIT = 40 * 1024 * 1024


def iota(shape, axis):
    return lax.broadcasted_iota(jnp.int32, shape, axis)


def one_hot(mask):
    return jnp.where(mask, 1.0, 0.0).astype(jnp.bfloat16)


def halo_offset(index, width):
    return jnp.where(index < 2, index - 2, index - 2 + width)


def wrapped(index, count):
    return jnp.where(index >= count, index - count, index)


def columns(harms, blocks, first):
    shape = (harms * LANES, blocks * LANES)
    row, col = iota(shape, 0), iota(shape, 1)
    owner = wrapped(col // LANES + first, blocks)
    return row // LANES, row % LANES, owner, col % LANES


def side_by_side(ref, group, rows):
    return jnp.concatenate([ref[k, group, rows, :] for k in range(ref.shape[0])], axis=1)


def matrix_kernel(sizes, groups, mode, rad, main_m, halo_m):
    harms, blocks, width = sizes
    harm_in, cell_in, owner, lane = columns(harms, blocks, mode[0])
    main_m[...] = one_hot(
        (lane // width == harm_in) & (cell_in == owner * width + lane % width)
    )
    shift = jnp.where(rad[0] == 0, LANES, -LANES)
    depth = harms * LANES
    span_h = harms * HALO
    part = lane % span_h
    wanted = owner * width + halo_offset(part % HALO, width)
    same = (part // HALO == harm_in) & (lane < groups * span_h)
    halo_m[0:depth, :] = one_hot(same & (cell_in == wanted))
    halo_m[depth:, :] = one_hot(same & (cell_in + shift == wanted))


def pack_kernel(sizes, cells, slots, own_d, own_a, far_d, far_a, main_m, halo_m, *outs):
    harms, blocks, width = sizes
    groups, group_rows = own_d.shape[1], own_d.shape[2]
    fields = group_rows // cells
    tile = groups * cells
    lane_group = (iota((group_rows, blocks * LANES), 1) % LANES) // (harms * HALO)
    everything = slice(0, group_rows)
    base = 2 * fields * tile
    for array, (own, far) in enumerate(((own_d, far_d), (own_a, far_a))):
        near = [side_by_side(own, group, everything) for group in range(groups)]
        rows = [
            near[group][field * cells : (field + 1) * cells, :]
            for field in range(fields)
            for group in range(groups)
        ]
        main = jnp.dot(
            jnp.concatenate(rows, axis=0), main_m[...], preferred_element_type=jnp.float32
        )
        pieces = [
            jnp.concatenate([near[group], side_by_side(far, group, everything)], axis=1)
            for group in range(groups)
        ]
        ends = jnp.dot(
            jnp.concatenate(pieces, axis=0), halo_m[...], preferred_element_type=jnp.float32
        )
        held = jnp.zeros((group_rows, blocks * LANES), jnp.float32)
        for group in range(groups):
            held = jnp.where(
                lane_group == group, ends[group * group_rows : (group + 1) * group_rows], held
            )
        for step, out in enumerate(outs):
            lanes = slice(step * LANES, (step + 1) * LANES)
            start = array * fields * tile
            out[start : start + fields * tile, :] = main[:, lanes].astype(jnp.bfloat16)
            start = base + array * group_rows
            out[start : start + group_rows, :] = held[:, lanes].astype(jnp.bfloat16)
    lane = iota((SLOT_ROWS, LANES), 1)
    listed = jnp.zeros((SLOT_ROWS, LANES), jnp.int32)
    for index in range(slots.shape[0]):
        listed = jnp.where(lane == index, slots[index], listed)
    for out in outs:
        out[base + 2 * group_rows :, :] = listed.astype(jnp.float32).astype(jnp.bfloat16)


def coefficient(distance):
    near = jnp.where(distance == 1, 8.0, jnp.where(distance == -1, -8.0, 0.0))
    return jnp.where(distance == 2, -1.0, jnp.where(distance == -2, 1.0, near))


def triad_kernel(sizes, mode, *refs):
    harms, blocks, width, groups, slots, count, cells, harm_devices = sizes
    mains = refs[:blocks]
    origins = [wrapped(mode[0] - step + blocks, blocks) for step in range(blocks)]
    out, radial_m, axial_m, plain_v, axial_v, radial_v, sums, slots_v, slots_s, slots_sem = refs[
        blocks:
    ]
    halo_row = 2 * count * groups * cells
    slot_row = halo_row + 2 * count * cells
    for step in range(blocks):
        slots_v[step : step + 1, :] = (
            mains[step][slot_row : slot_row + SLOT_ROWS, :].astype(jnp.float32)[0:1, :]
        ).astype(jnp.int32)
    listing = pltpu.make_async_copy(slots_v, slots_s, slots_sem)
    listing.start()
    span_h = harms * HALO
    used = harms * width
    tile = groups * cells
    shape = (LANES, LANES)
    row, col = iota(shape, 0), iota(shape, 1)
    inside = (row // width == col // width) & (row < used) & (col < used)
    within = jnp.where(inside, coefficient(row - col), 0.0).astype(jnp.bfloat16)
    square = (tile, tile)
    row_t, col_t = iota(square, 0), iota(square, 1)
    axial_m[...] = jnp.where(
        row_t // cells == col_t // cells, coefficient(col_t - row_t), 0.0
    ).astype(jnp.bfloat16)

    for group in range(groups):
        part = row - group * span_h
        mine = (part >= 0) & (part < span_h) & (col < used) & (part // HALO == col // width)
        place = halo_offset(part % HALO, width)
        around = jnp.where(mine, coefficient(place - col % width), 0.0).astype(jnp.bfloat16)
        radial_m[group] = jnp.concatenate([within, around], axis=0)
    for group in range(groups):
        pieces = []
        for array in range(2):
            for local in range(count):
                for step in range(blocks):
                    start = ((array * count + local) * groups + group) * cells
                    beside = halo_row + (array * count + local) * cells
                    pieces.append(
                        jnp.concatenate(
                            [
                                mains[step][start : start + cells, :],
                                mains[step][beside : beside + cells, :],
                            ],
                            axis=1,
                        )
                    )
        slopes = jnp.dot(
            jnp.concatenate(pieces, axis=0), radial_m[group], preferred_element_type=jnp.float32
        )
        index = 0
        for array in range(2):
            for local in range(count):
                for step in range(blocks):
                    radial_v[array * count + local, origins[step] * groups + group] = slopes[
                        index * cells : (index + 1) * cells, :
                    ]
                    index += 1
    for step in range(blocks):
        for local in range(count):
            starts = [(array * count + local) * tile for array in range(2)]
            both = jnp.concatenate([mains[step][s : s + tile, :] for s in starts], axis=1)
            slopes = jnp.dot(axial_m[...], both, preferred_element_type=jnp.float32)
            for array in range(2):
                for group in range(groups):
                    axial_v[array * count + local, origins[step] * groups + group] = slopes[
                        group * cells : (group + 1) * cells, array * LANES : (array + 1) * LANES
                    ]
        for which in range(4):
            for group in range(groups):
                held = which // 2 * count + 1 + which % 2
                start = (held * groups + group) * cells
                plain_v[which, origins[step] * groups + group] = mains[step][
                    start : start + cells, :
                ].astype(jnp.float32)

    listing.wait()

    @pl.loop(0, blocks * slots)
    def _(index):
        step = index // slots
        listed = wrapped(mode[0] - step + blocks, blocks)
        entry = lax.rem(index, slots) * blocks

        def add_stop(stop, running):
            source = wrapped(step - stop + blocks, blocks)
            at_a = step * groups + slots_s[listed, (entry + stop) * 2] * 2
            at_d = source * groups + slots_s[listed, (entry + stop) * 2 + 1] * 2
            d1r, d1i, d2r, d2i = (plain_v[w, at_d + c] for w in (0, 1) for c in (0, 1))
            a1r, a1i, a2r, a2i = (plain_v[w, at_a + c] for w in (2, 3) for c in (0, 1))
            result = []
            for local in range(count):
                xar, xai = axial_v[count + local, at_a], axial_v[count + local, at_a + 1]
                rar, rai = radial_v[count + local, at_a], radial_v[count + local, at_a + 1]
                xdr, xdi = axial_v[local, at_d], axial_v[local, at_d + 1]
                rdr, rdi = radial_v[local, at_d], radial_v[local, at_d + 1]
                real = (d1r * xar + d1i * xai) + (d2r * rar + d2i * rai)
                real = real + ((xdr * a1r + xdi * a1i) + (rdr * a2r + rdi * a2i))
                imag = (d1r * xai - d1i * xar) + (d2r * rai - d2i * rar)
                imag = imag + ((xdr * a1i - xdi * a1r) + (rdr * a2i - rdi * a2r))
                old_real, old_imag = running[local]
                result.append((old_real + real, old_imag + imag))
            return tuple(result)

        zero = jnp.zeros((cells, LANES), jnp.float32)
        running = tuple((zero, zero) for _ in range(count))
        if blocks <= 4:
            for stop in range(blocks):
                running = add_stop(stop, running)
        else:
            running = lax.fori_loop(0, blocks, add_stop, running)
        for local in range(count):
            for part in range(2):
                sums[index, part * count + local] = running[local][part]

    scale = 1.0 / (12.0 * math.sqrt(8.0 * blocks * HARMS))
    per_harm = blocks // harm_devices
    own_cells = cells // blocks
    lane_slot = iota((cells, LANES), 1) // width

    @pl.loop(0, blocks)
    def _(step):
        for row in range(2 * count):
            packed = jnp.zeros((cells, LANES), jnp.float32)
            for slot in range(slots):
                value = sums[step * slots + slot, row]
                reach = harms // 2
                while reach:
                    value = value + pltpu.roll(value, reach * width, axis=1)
                    reach //= 2
                if used < LANES and slot:
                    value = pltpu.roll(value, slot * width, axis=1)
                packed = jnp.where(lane_slot == slot, value, packed)
            packed = packed * scale
            for owner in range(blocks):
                out[
                    owner * harm_devices + step // per_harm,
                    lax.rem(step, per_harm),
                    row * own_cells : (row + 1) * own_cells,
                    :,
                ] = packed[owner * own_cells : (owner + 1) * own_cells, :]


def unpack_kernel(sizes, came, out_ref):
    blocks, harm_devices, slots, width, per_harm = sizes
    rows = came.shape[2]
    lane_block = iota((rows, LANES), 1) // width
    for local in range(per_harm):
        packed = [jnp.zeros((rows, LANES), jnp.float32) for _ in range(slots)]
        for source in range(blocks):
            total = came[source * harm_devices, local]
            for harm in range(1, harm_devices):
                total = total + came[source * harm_devices + harm, local]
            for slot in range(slots):
                amount = (source - slot) * width % LANES
                moved = pltpu.roll(total, amount, axis=1) if amount else total
                packed[slot] = jnp.where(lane_block == source, moved, packed[slot])
        for slot in range(slots):
            out_ref[local * slots + slot] = packed[slot]


def smem(count):
    return [pl.BlockSpec(memory_space=pltpu.SMEM)] * count


def vmem(count):
    return [pl.BlockSpec(memory_space=pltpu.VMEM)] * count


def moved_up(values, axis):
    count = lax.axis_size(axis)
    result = [values[0]]
    for step in range(1, count):
        pairs = [(source, (source + step) % count) for source in range(count)]
        result.append(lax.ppermute(values[step], axis, pairs))
    return result


def body(direct_field, adjoint_field, triad_slots):
    blocks, harm_devices = lax.axis_size("mode"), lax.axis_size("harm")
    harms, slots, parts, fields, cells, radial = direct_field.shape
    width = radial // blocks
    groups, group_rows = slots * parts, fields * cells
    tile = groups * cells
    params = pltpu.CompilerParams(vmem_limit_bytes=VMEM_LIMIT)
    mode, rad = (lax.axis_index(axis).astype(jnp.int32).reshape(1) for axis in ("mode", "rad"))

    direct = direct_field.reshape(harms, groups, group_rows, radial)
    adjoint = adjoint_field.reshape(harms, groups, group_rows, radial)
    swap = [(0, 1), (1, 0)]
    far_direct = lax.ppermute(direct, "rad", swap)
    far_adjoint = lax.ppermute(adjoint, "rad", swap)

    sizes = (harms, blocks, width)
    depth, span = harms * LANES, blocks * LANES
    matrices = pl.pallas_call(
        functools.partial(matrix_kernel, sizes, groups),
        out_shape=[
            jax.ShapeDtypeStruct((depth, span), jnp.bfloat16),
            jax.ShapeDtypeStruct((2 * depth, span), jnp.bfloat16),
        ],
        in_specs=smem(2),
        out_specs=vmem(2),
        compiler_params=params,
        name="matrices",
    )(mode, rad)
    payload_rows = 2 * fields * tile + 2 * group_rows + SLOT_ROWS
    slabs = pl.pallas_call(
        functools.partial(pack_kernel, sizes, cells),
        out_shape=[jax.ShapeDtypeStruct((payload_rows, LANES), jnp.bfloat16)] * blocks,
        in_specs=smem(1) + vmem(6),
        out_specs=vmem(blocks),
        compiler_params=params,
        name="pack",
    )(triad_slots.reshape(-1), direct, adjoint, far_direct, far_adjoint, *matrices)
    came = moved_up(slabs, "mode")

    per_harm, own_cells = blocks // harm_devices, cells // blocks
    sizes = (harms, blocks, width, groups, slots, fields, cells, harm_devices)
    listed = (max(blocks, 8), LANES)
    derived = pltpu.VMEM((2 * fields, blocks * groups, cells, LANES), jnp.float32)
    out_rows = 2 * fields * own_cells
    sent = pl.pallas_call(
        functools.partial(triad_kernel, sizes),
        out_shape=jax.ShapeDtypeStruct(
            (blocks * harm_devices, per_harm, out_rows, LANES), jnp.float32
        ),
        in_specs=smem(1) + vmem(blocks),
        out_specs=vmem(1)[0],
        scratch_shapes=[
            pltpu.VMEM((groups, 2 * LANES, LANES), jnp.bfloat16),
            pltpu.VMEM((tile, tile), jnp.bfloat16),
            pltpu.VMEM((4, blocks * groups, cells, LANES), jnp.float32),
            derived,
            derived,
            pltpu.VMEM((blocks * slots, 2 * fields, cells, LANES), jnp.float32),
            pltpu.VMEM(listed, jnp.int32),
            pltpu.SMEM(listed, jnp.int32),
            pltpu.SemaphoreType.DMA,
        ],
        compiler_params=params,
        name="triads",
    )(mode, *came)
    owned = lax.all_to_all(sent, ("mode", "harm"), split_axis=0, concat_axis=0, tiled=True)

    result = pl.pallas_call(
        functools.partial(unpack_kernel, (blocks, harm_devices, slots, width, per_harm)),
        out_shape=jax.ShapeDtypeStruct((per_harm * slots, out_rows, LANES), jnp.float32),
        in_specs=vmem(1),
        out_specs=vmem(1)[0],
        compiler_params=params,
        name="unpack",
    )(owned)
    return result.reshape(per_harm * slots, 2, fields, own_cells, radial)


def solution(mesh):
    return jax.shard_map(
        body,
        mesh=mesh,
        in_specs=(
            P(("case", "harm"), "mode", None, None, None, "rad"),
            P(("case", "harm"), "mode", None, None, None, "rad"),
            P("mode", None, None),
        ),
        out_specs=P(("case", "harm"), None, None, "mode", "rad"),
        check_vma=False,
    )
```

```python
import functools
import math

import jax
import jax.numpy as jnp
from jax import lax
from jax.experimental import pallas as pl
from jax.experimental.pallas import tpu as pltpu
from jax.sharding import PartitionSpec as P

HARMS = 8
LANES = 128
HALO = 4
SLOT_ROWS = 16
VMEM_LIMIT = 40 * 1024 * 1024


def iota(shape, axis):
    return lax.broadcasted_iota(jnp.int32, shape, axis)


def one_hot(mask):
    return jnp.where(mask, 1.0, 0.0).astype(jnp.bfloat16)


def halo_offset(index, width):
    return jnp.where(index < 2, index - 2, index - 2 + width)


def wrapped(index, count):
    return jnp.where(index >= count, index - count, index)


def columns(harms, blocks, first):
    shape = (harms * LANES, blocks * LANES)
    row, col = iota(shape, 0), iota(shape, 1)
    owner = wrapped(col // LANES + first, blocks)
    return row // LANES, row % LANES, owner, col % LANES


def side_by_side(ref, group, rows):
    return jnp.concatenate([ref[k, group, rows, :] for k in range(ref.shape[0])], axis=1)


def matrix_kernel(sizes, groups, mode, rad, _direct, _adjoint, main_m, halo_m):
    harms, blocks, width = sizes
    harm_in, cell_in, owner, lane = columns(harms, blocks, mode[0])
    main_m[...] = one_hot(
        (lane // width == harm_in) & (cell_in == owner * width + lane % width)
    )
    shift = jnp.where(rad[0] == 0, LANES, -LANES)
    depth = harms * LANES
    span_h = harms * HALO
    part = lane % span_h
    wanted = owner * width + halo_offset(part % HALO, width)
    same = (part // HALO == harm_in) & (lane < groups * span_h)
    halo_m[0:depth, :] = one_hot(same & (cell_in == wanted))
    halo_m[depth:, :] = one_hot(same & (cell_in + shift == wanted))


def pack_kernel(sizes, cells, slots, own_d, own_a, far_d, far_a, main_m, halo_m, *outs):
    harms, blocks, width = sizes
    groups, group_rows = own_d.shape[1], own_d.shape[2]
    fields = group_rows // cells
    tile = groups * cells
    lane_group = (iota((group_rows, blocks * LANES), 1) % LANES) // (harms * HALO)
    everything = slice(0, group_rows)
    base = 2 * fields * tile
    for array, (own, far) in enumerate(((own_d, far_d), (own_a, far_a))):
        near = [side_by_side(own, group, everything) for group in range(groups)]
        rows = [
            near[group][field * cells : (field + 1) * cells, :]
            for field in range(fields)
            for group in range(groups)
        ]
        main = jnp.dot(
            jnp.concatenate(rows, axis=0), main_m[...], preferred_element_type=jnp.float32
        )
        pieces = [
            jnp.concatenate([near[group], side_by_side(far, group, everything)], axis=1)
            for group in range(groups)
        ]
        ends = jnp.dot(
            jnp.concatenate(pieces, axis=0), halo_m[...], preferred_element_type=jnp.float32
        )
        held = jnp.zeros((group_rows, blocks * LANES), jnp.float32)
        for group in range(groups):
            held = jnp.where(
                lane_group == group, ends[group * group_rows : (group + 1) * group_rows], held
            )
        for step, out in enumerate(outs):
            lanes = slice(step * LANES, (step + 1) * LANES)
            start = array * fields * tile
            out[start : start + fields * tile, :] = main[:, lanes].astype(jnp.bfloat16)
            start = base + array * group_rows
            out[start : start + group_rows, :] = held[:, lanes].astype(jnp.bfloat16)
    lane = iota((SLOT_ROWS, LANES), 1)
    listed = jnp.zeros((SLOT_ROWS, LANES), jnp.int32)
    for index in range(slots.shape[0]):
        listed = jnp.where(lane == index, slots[index], listed)
    for out in outs:
        out[base + 2 * group_rows :, :] = listed.astype(jnp.float32).astype(jnp.bfloat16)


def coefficient(distance):
    near = jnp.where(distance == 1, 8.0, jnp.where(distance == -1, -8.0, 0.0))
    return jnp.where(distance == 2, -1.0, jnp.where(distance == -2, 1.0, near))


def triad_kernel(sizes, mode, *refs):
    harms, blocks, width, groups, slots, count, cells, harm_devices = sizes
    mains = refs[:blocks]
    origins = [wrapped(mode[0] - step + blocks, blocks) for step in range(blocks)]
    out, radial_m, axial_m, plain_v, axial_v, radial_v, sums, slots_v, slots_s, slots_sem = refs[
        blocks:
    ]
    halo_row = 2 * count * groups * cells
    slot_row = halo_row + 2 * count * cells
    for step in range(blocks):
        slots_v[step : step + 1, :] = (
            mains[step][slot_row : slot_row + SLOT_ROWS, :].astype(jnp.float32)[0:1, :]
        ).astype(jnp.int32)
    listing = pltpu.make_async_copy(slots_v, slots_s, slots_sem)
    listing.start()
    span_h = harms * HALO
    used = harms * width
    tile = groups * cells
    shape = (LANES, LANES)
    row, col = iota(shape, 0), iota(shape, 1)
    inside = (row // width == col // width) & (row < used) & (col < used)
    within = jnp.where(inside, coefficient(row - col), 0.0).astype(jnp.bfloat16)
    square = (tile, tile)
    row_t, col_t = iota(square, 0), iota(square, 1)
    axial_m[...] = jnp.where(
        row_t // cells == col_t // cells, coefficient(col_t - row_t), 0.0
    ).astype(jnp.bfloat16)

    for group in range(groups):
        part = row - group * span_h
        mine = (part >= 0) & (part < span_h) & (col < used) & (part // HALO == col // width)
        place = halo_offset(part % HALO, width)
        around = jnp.where(mine, coefficient(place - col % width), 0.0).astype(jnp.bfloat16)
        radial_m[group] = jnp.concatenate([within, around], axis=0)
    for group in range(groups):
        pieces = []
        for array in range(2):
            for local in range(count):
                for step in range(blocks):
                    start = ((array * count + local) * groups + group) * cells
                    beside = halo_row + (array * count + local) * cells
                    pieces.append(
                        jnp.concatenate(
                            [
                                mains[step][start : start + cells, :],
                                mains[step][beside : beside + cells, :],
                            ],
                            axis=1,
                        )
                    )
        slopes = jnp.dot(
            jnp.concatenate(pieces, axis=0), radial_m[group], preferred_element_type=jnp.float32
        )
        index = 0
        for array in range(2):
            for local in range(count):
                for step in range(blocks):
                    radial_v[array * count + local, origins[step] * groups + group] = slopes[
                        index * cells : (index + 1) * cells, :
                    ]
                    index += 1
    for step in range(blocks):
        for local in range(count):
            starts = [(array * count + local) * tile for array in range(2)]
            both = jnp.concatenate([mains[step][s : s + tile, :] for s in starts], axis=1)
            slopes = jnp.dot(axial_m[...], both, preferred_element_type=jnp.float32)
            for array in range(2):
                for group in range(groups):
                    axial_v[array * count + local, origins[step] * groups + group] = slopes[
                        group * cells : (group + 1) * cells, array * LANES : (array + 1) * LANES
                    ]
        for which in range(4):
            for group in range(groups):
                held = which // 2 * count + 1 + which % 2
                start = (held * groups + group) * cells
                plain_v[which, origins[step] * groups + group] = mains[step][
                    start : start + cells, :
                ].astype(jnp.float32)

    listing.wait()

    @pl.loop(0, blocks * slots)
    def _(index):
        step = index // slots
        listed = wrapped(mode[0] - step + blocks, blocks)
        entry = lax.rem(index, slots) * blocks

        def add_stop(stop, running):
            source = wrapped(step - stop + blocks, blocks)
            at_a = step * groups + slots_s[listed, (entry + stop) * 2] * 2
            at_d = source * groups + slots_s[listed, (entry + stop) * 2 + 1] * 2
            d1r, d1i, d2r, d2i = (plain_v[w, at_d + c] for w in (0, 1) for c in (0, 1))
            a1r, a1i, a2r, a2i = (plain_v[w, at_a + c] for w in (2, 3) for c in (0, 1))
            result = []
            for local in range(count):
                xar, xai = axial_v[count + local, at_a], axial_v[count + local, at_a + 1]
                rar, rai = radial_v[count + local, at_a], radial_v[count + local, at_a + 1]
                xdr, xdi = axial_v[local, at_d], axial_v[local, at_d + 1]
                rdr, rdi = radial_v[local, at_d], radial_v[local, at_d + 1]
                real = (d1r * xar + d1i * xai) + (d2r * rar + d2i * rai)
                real = real + ((xdr * a1r + xdi * a1i) + (rdr * a2r + rdi * a2i))
                imag = (d1r * xai - d1i * xar) + (d2r * rai - d2i * rar)
                imag = imag + ((xdr * a1i - xdi * a1r) + (rdr * a2i - rdi * a2r))
                old_real, old_imag = running[local]
                result.append((old_real + real, old_imag + imag))
            return tuple(result)

        zero = jnp.zeros((cells, LANES), jnp.float32)
        running = tuple((zero, zero) for _ in range(count))
        if blocks <= 4:
            for stop in range(blocks):
                running = add_stop(stop, running)
        else:
            running = lax.fori_loop(0, blocks, add_stop, running)
        for local in range(count):
            for part in range(2):
                sums[index, part * count + local] = running[local][part]

    scale = 1.0 / (12.0 * math.sqrt(8.0 * blocks * HARMS))
    per_harm = blocks // harm_devices
    own_cells = cells // blocks
    lane_slot = iota((cells, LANES), 1) // width

    @pl.loop(0, blocks)
    def _(step):
        for row in range(2 * count):
            packed = jnp.zeros((cells, LANES), jnp.float32)
            for slot in range(slots):
                value = sums[step * slots + slot, row]
                reach = harms // 2
                while reach:
                    value = value + pltpu.roll(value, reach * width, axis=1)
                    reach //= 2
                if used < LANES and slot:
                    value = pltpu.roll(value, slot * width, axis=1)
                packed = jnp.where(lane_slot == slot, value, packed)
            packed = packed * scale
            for owner in range(blocks):
                out[
                    owner * harm_devices + step // per_harm,
                    lax.rem(step, per_harm),
                    row * own_cells : (row + 1) * own_cells,
                    :,
                ] = packed[owner * own_cells : (owner + 1) * own_cells, :]


def unpack_kernel(sizes, came, out_ref):
    blocks, harm_devices, slots, width, per_harm = sizes
    rows = came.shape[2]
    lane_block = iota((rows, LANES), 1) // width
    for local in range(per_harm):
        packed = [jnp.zeros((rows, LANES), jnp.float32) for _ in range(slots)]
        for source in range(blocks):
            total = came[source * harm_devices, local]
            for harm in range(1, harm_devices):
                total = total + came[source * harm_devices + harm, local]
            for slot in range(slots):
                amount = (source - slot) * width % LANES
                moved = pltpu.roll(total, amount, axis=1) if amount else total
                packed[slot] = jnp.where(lane_block == source, moved, packed[slot])
        for slot in range(slots):
            out_ref[local * slots + slot] = packed[slot]


def smem(count):
    return [pl.BlockSpec(memory_space=pltpu.SMEM)] * count


def vmem(count):
    return [pl.BlockSpec(memory_space=pltpu.VMEM)] * count


def moved_up(values, axis):
    count = lax.axis_size(axis)
    result = [values[0]]
    for step in range(1, count):
        pairs = [(source, (source + step) % count) for source in range(count)]
        result.append(lax.ppermute(values[step], axis, pairs))
    return result


def body(direct_field, adjoint_field, triad_slots):
    blocks, harm_devices = lax.axis_size("mode"), lax.axis_size("harm")
    harms, slots, parts, fields, cells, radial = direct_field.shape
    width = radial // blocks
    groups, group_rows = slots * parts, fields * cells
    tile = groups * cells
    params = pltpu.CompilerParams(vmem_limit_bytes=VMEM_LIMIT)
    mode, rad = (lax.axis_index(axis).astype(jnp.int32).reshape(1) for axis in ("mode", "rad"))

    direct = direct_field.reshape(harms, groups, group_rows, radial)
    adjoint = adjoint_field.reshape(harms, groups, group_rows, radial)
    swap = [(0, 1), (1, 0)]
    far_direct = lax.ppermute(direct, "rad", swap)
    far_adjoint = lax.ppermute(adjoint, "rad", swap)

    sizes = (harms, blocks, width)
    depth, span = harms * LANES, blocks * LANES
    matrices = pl.pallas_call(
        functools.partial(matrix_kernel, sizes, groups),
        out_shape=[
            jax.ShapeDtypeStruct((depth, span), jnp.bfloat16),
            jax.ShapeDtypeStruct((2 * depth, span), jnp.bfloat16),
        ],
        in_specs=smem(2) + vmem(2),
        out_specs=vmem(2),
        compiler_params=params,
        name="matrices",
    )(mode, rad, direct, adjoint)
    payload_rows = 2 * fields * tile + 2 * group_rows + SLOT_ROWS
    slabs = pl.pallas_call(
        functools.partial(pack_kernel, sizes, cells),
        out_shape=[jax.ShapeDtypeStruct((payload_rows, LANES), jnp.bfloat16)] * blocks,
        in_specs=smem(1) + vmem(6),
        out_specs=vmem(blocks),
        compiler_params=params,
        name="pack",
    )(triad_slots.reshape(-1), direct, adjoint, far_direct, far_adjoint, *matrices)
    came = moved_up(slabs, "mode")

    per_harm, own_cells = blocks // harm_devices, cells // blocks
    sizes = (harms, blocks, width, groups, slots, fields, cells, harm_devices)
    listed = (max(blocks, 8), LANES)
    derived = pltpu.VMEM((2 * fields, blocks * groups, cells, LANES), jnp.float32)
    out_rows = 2 * fields * own_cells
    sent = pl.pallas_call(
        functools.partial(triad_kernel, sizes),
        out_shape=jax.ShapeDtypeStruct(
            (blocks * harm_devices, per_harm, out_rows, LANES), jnp.float32
        ),
        in_specs=smem(1) + vmem(blocks),
        out_specs=vmem(1)[0],
        scratch_shapes=[
            pltpu.VMEM((groups, 2 * LANES, LANES), jnp.bfloat16),
            pltpu.VMEM((tile, tile), jnp.bfloat16),
            pltpu.VMEM((4, blocks * groups, cells, LANES), jnp.float32),
            derived,
            derived,
            pltpu.VMEM((blocks * slots, 2 * fields, cells, LANES), jnp.float32),
            pltpu.VMEM(listed, jnp.int32),
            pltpu.SMEM(listed, jnp.int32),
            pltpu.SemaphoreType.DMA,
        ],
        compiler_params=params,
        name="triads",
    )(mode, *came)
    owned = lax.all_to_all(sent, ("mode", "harm"), split_axis=0, concat_axis=0, tiled=True)

    result = pl.pallas_call(
        functools.partial(unpack_kernel, (blocks, harm_devices, slots, width, per_harm)),
        out_shape=jax.ShapeDtypeStruct((per_harm * slots, out_rows, LANES), jnp.float32),
        in_specs=vmem(1),
        out_specs=vmem(1)[0],
        compiler_params=params,
        name="unpack",
    )(owned)
    return result.reshape(per_harm * slots, 2, fields, own_cells, radial)


def solution(mesh):
    return jax.shard_map(
        body,
        mesh=mesh,
        in_specs=(
            P(("case", "harm"), "mode", None, None, None, "rad"),
            P(("case", "harm"), "mode", None, None, None, "rad"),
            P("mode", None, None),
        ),
        out_specs=P(("case", "harm"), None, None, "mode", "rad"),
        check_vma=False,
    )
```

```python
import functools
import itertools
import math

import jax
import jax.numpy as jnp
from jax import lax
from jax.experimental import pallas as pl
from jax.experimental.pallas import tpu as pltpu
from jax.sharding import PartitionSpec as P

HARMS = 8
LANES = 128
HALO = 4
SLOT_ROWS = 16
VMEM_LIMIT = 40 * 1024 * 1024


def iota(shape, axis):
    return lax.broadcasted_iota(jnp.int32, shape, axis)


def one_hot(mask):
    return jnp.where(mask, 1.0, 0.0).astype(jnp.bfloat16)


def halo_offset(index, width):
    return jnp.where(index < 2, index - 2, index - 2 + width)


def wrapped(index, count):
    return jnp.where(index >= count, index - count, index)


def columns(harms, blocks, first):
    shape = (harms * LANES, blocks * LANES)
    row, col = iota(shape, 0), iota(shape, 1)
    owner = wrapped(col // LANES + first, blocks)
    return row // LANES, row % LANES, owner, col % LANES


def side_by_side(ref, group, rows):
    return jnp.concatenate([ref[k, group, rows, :] for k in range(ref.shape[0])], axis=1)


def matrix_kernel(sizes, groups, mode, rad, _direct, _adjoint, main_m, halo_m):
    harms, blocks, width = sizes
    harm_in, cell_in, owner, lane = columns(harms, blocks, mode[0])
    main_m[...] = one_hot(
        (lane // width == harm_in) & (cell_in == owner * width + lane % width)
    )
    shift = jnp.where(rad[0] == 0, LANES, -LANES)
    depth = harms * LANES
    span_h = harms * HALO
    part = lane % span_h
    wanted = owner * width + halo_offset(part % HALO, width)
    same = (part // HALO == harm_in) & (lane < groups * span_h)
    halo_m[0:depth, :] = one_hot(same & (cell_in == wanted))
    halo_m[depth:, :] = one_hot(same & (cell_in + shift == wanted))


def pack_kernel(sizes, cells, slots, own_d, own_a, far_d, far_a, main_m, halo_m, *outs):
    harms, blocks, width = sizes
    groups, group_rows = own_d.shape[1], own_d.shape[2]
    fields = group_rows // cells
    tile = groups * cells
    lane_group = (iota((group_rows, blocks * LANES), 1) % LANES) // (harms * HALO)
    everything = slice(0, group_rows)
    base = 2 * fields * tile
    for array, (own, far) in enumerate(((own_d, far_d), (own_a, far_a))):
        near = [side_by_side(own, group, everything) for group in range(groups)]
        rows = [
            near[group][field * cells : (field + 1) * cells, :]
            for field in range(fields)
            for group in range(groups)
        ]
        main = jnp.dot(
            jnp.concatenate(rows, axis=0), main_m[...], preferred_element_type=jnp.float32
        )
        pieces = [
            jnp.concatenate([near[group], side_by_side(far, group, everything)], axis=1)
            for group in range(groups)
        ]
        ends = jnp.dot(
            jnp.concatenate(pieces, axis=0), halo_m[...], preferred_element_type=jnp.float32
        )
        held = jnp.zeros((group_rows, blocks * LANES), jnp.float32)
        for group in range(groups):
            held = jnp.where(
                lane_group == group, ends[group * group_rows : (group + 1) * group_rows], held
            )
        for step, out in enumerate(outs):
            lanes = slice(step * LANES, (step + 1) * LANES)
            start = array * fields * tile
            out[start : start + fields * tile, :] = main[:, lanes].astype(jnp.bfloat16)
            start = base + array * group_rows
            out[start : start + group_rows, :] = held[:, lanes].astype(jnp.bfloat16)
    lane = iota((SLOT_ROWS, LANES), 1)
    listed = jnp.zeros((SLOT_ROWS, LANES), jnp.int32)
    for at, which, stop in itertools.product(*map(range, slots.shape)):
        index = (at * slots.shape[2] + stop) * 2 + which
        listed = jnp.where(lane == index, slots[at, which, stop], listed)
    for out in outs:
        out[base + 2 * group_rows :, :] = listed.astype(jnp.float32).astype(jnp.bfloat16)


def coefficient(distance):
    near = jnp.where(distance == 1, 8.0, jnp.where(distance == -1, -8.0, 0.0))
    return jnp.where(distance == 2, -1.0, jnp.where(distance == -2, 1.0, near))


def triad_kernel(sizes, mode, *refs):
    harms, blocks, width, groups, slots, count, cells, harm_devices = sizes
    mains = refs[:blocks]
    origins = [wrapped(mode[0] - step + blocks, blocks) for step in range(blocks)]
    out, radial_m, axial_m, plain_v, axial_v, radial_v, sums, slots_v, slots_s, slots_sem = refs[
        blocks:
    ]
    halo_row = 2 * count * groups * cells
    slot_row = halo_row + 2 * count * cells
    for step in range(blocks):
        slots_v[step : step + 1, :] = (
            mains[step][slot_row : slot_row + SLOT_ROWS, :].astype(jnp.float32)[0:1, :]
        ).astype(jnp.int32)
    listing = pltpu.make_async_copy(slots_v, slots_s, slots_sem)
    listing.start()
    span_h = harms * HALO
    used = harms * width
    tile = groups * cells
    shape = (LANES, LANES)
    row, col = iota(shape, 0), iota(shape, 1)
    inside = (row // width == col // width) & (row < used) & (col < used)
    within = jnp.where(inside, coefficient(row - col), 0.0).astype(jnp.bfloat16)
    square = (tile, tile)
    row_t, col_t = iota(square, 0), iota(square, 1)
    axial_m[...] = jnp.where(
        row_t // cells == col_t // cells, coefficient(col_t - row_t), 0.0
    ).astype(jnp.bfloat16)

    for group in range(groups):
        part = row - group * span_h
        mine = (part >= 0) & (part < span_h) & (col < used) & (part // HALO == col // width)
        place = halo_offset(part % HALO, width)
        around = jnp.where(mine, coefficient(place - col % width), 0.0).astype(jnp.bfloat16)
        radial_m[group] = jnp.concatenate([within, around], axis=0)
    for group in range(groups):
        pieces = []
        for array in range(2):
            for local in range(count):
                for step in range(blocks):
                    start = ((array * count + local) * groups + group) * cells
                    beside = halo_row + (array * count + local) * cells
                    pieces.append(
                        jnp.concatenate(
                            [
                                mains[step][start : start + cells, :],
                                mains[step][beside : beside + cells, :],
                            ],
                            axis=1,
                        )
                    )
        slopes = jnp.dot(
            jnp.concatenate(pieces, axis=0), radial_m[group], preferred_element_type=jnp.float32
        )
        index = 0
        for array in range(2):
            for local in range(count):
                for step in range(blocks):
                    radial_v[array * count + local, origins[step] * groups + group] = slopes[
                        index * cells : (index + 1) * cells, :
                    ]
                    index += 1
    for step in range(blocks):
        for local in range(count):
            starts = [(array * count + local) * tile for array in range(2)]
            both = jnp.concatenate([mains[step][s : s + tile, :] for s in starts], axis=1)
            slopes = jnp.dot(axial_m[...], both, preferred_element_type=jnp.float32)
            for array in range(2):
                for group in range(groups):
                    axial_v[array * count + local, origins[step] * groups + group] = slopes[
                        group * cells : (group + 1) * cells, array * LANES : (array + 1) * LANES
                    ]
        for which in range(4):
            for group in range(groups):
                held = which // 2 * count + 1 + which % 2
                start = (held * groups + group) * cells
                plain_v[which, origins[step] * groups + group] = mains[step][
                    start : start + cells, :
                ].astype(jnp.float32)

    listing.wait()

    @pl.loop(0, blocks * slots)
    def _(index):
        step = index // slots
        listed = wrapped(mode[0] - step + blocks, blocks)
        entry = lax.rem(index, slots) * blocks

        def add_stop(stop, running):
            source = wrapped(step - stop + blocks, blocks)
            at_a = step * groups + slots_s[listed, (entry + stop) * 2] * 2
            at_d = source * groups + slots_s[listed, (entry + stop) * 2 + 1] * 2
            d1r, d1i, d2r, d2i = (plain_v[w, at_d + c] for w in (0, 1) for c in (0, 1))
            a1r, a1i, a2r, a2i = (plain_v[w, at_a + c] for w in (2, 3) for c in (0, 1))
            result = []
            for local in range(count):
                xar, xai = axial_v[count + local, at_a], axial_v[count + local, at_a + 1]
                rar, rai = radial_v[count + local, at_a], radial_v[count + local, at_a + 1]
                xdr, xdi = axial_v[local, at_d], axial_v[local, at_d + 1]
                rdr, rdi = radial_v[local, at_d], radial_v[local, at_d + 1]
                real = (d1r * xar + d1i * xai) + (d2r * rar + d2i * rai)
                real = real + ((xdr * a1r + xdi * a1i) + (rdr * a2r + rdi * a2i))
                imag = (d1r * xai - d1i * xar) + (d2r * rai - d2i * rar)
                imag = imag + ((xdr * a1i - xdi * a1r) + (rdr * a2i - rdi * a2r))
                old_real, old_imag = running[local]
                result.append((old_real + real, old_imag + imag))
            return tuple(result)

        zero = jnp.zeros((cells, LANES), jnp.float32)
        running = tuple((zero, zero) for _ in range(count))
        if blocks <= 4:
            for stop in range(blocks):
                running = add_stop(stop, running)
        else:
            running = lax.fori_loop(0, blocks, add_stop, running)
        for local in range(count):
            for part in range(2):
                sums[index, part * count + local] = running[local][part]

    scale = 1.0 / (12.0 * math.sqrt(8.0 * blocks * HARMS))
    per_harm = blocks // harm_devices
    own_cells = cells // blocks
    lane_slot = iota((cells, LANES), 1) // width

    @pl.loop(0, blocks)
    def _(step):
        for row in range(2 * count):
            packed = jnp.zeros((cells, LANES), jnp.float32)
            for slot in range(slots):
                value = sums[step * slots + slot, row]
                reach = harms // 2
                while reach:
                    value = value + pltpu.roll(value, reach * width, axis=1)
                    reach //= 2
                if used < LANES and slot:
                    value = pltpu.roll(value, slot * width, axis=1)
                packed = jnp.where(lane_slot == slot, value, packed)
            packed = packed * scale
            for owner in range(blocks):
                out[
                    owner * harm_devices + step // per_harm,
                    lax.rem(step, per_harm),
                    row * own_cells : (row + 1) * own_cells,
                    :,
                ] = packed[owner * own_cells : (owner + 1) * own_cells, :]


def unpack_kernel(sizes, came, out_ref):
    blocks, harm_devices, slots, width, per_harm = sizes
    rows = came.shape[2]
    lane_block = iota((rows, LANES), 1) // width
    for local in range(per_harm):
        packed = [jnp.zeros((rows, LANES), jnp.float32) for _ in range(slots)]
        for source in range(blocks):
            total = came[source * harm_devices, local]
            for harm in range(1, harm_devices):
                total = total + came[source * harm_devices + harm, local]
            for slot in range(slots):
                amount = (source - slot) * width % LANES
                moved = pltpu.roll(total, amount, axis=1) if amount else total
                packed[slot] = jnp.where(lane_block == source, moved, packed[slot])
        for slot in range(slots):
            out_ref[local * slots + slot] = packed[slot]


def smem(count):
    return [pl.BlockSpec(memory_space=pltpu.SMEM)] * count


def vmem(count):
    return [pl.BlockSpec(memory_space=pltpu.VMEM)] * count


def moved_up(values, axis):
    count = lax.axis_size(axis)
    result = [values[0]]
    for step in range(1, count):
        pairs = [(source, (source + step) % count) for source in range(count)]
        result.append(lax.ppermute(values[step], axis, pairs))
    return result


def body(direct_field, adjoint_field, triad_slots):
    blocks, harm_devices = lax.axis_size("mode"), lax.axis_size("harm")
    harms, slots, parts, fields, cells, radial = direct_field.shape
    width = radial // blocks
    groups, group_rows = slots * parts, fields * cells
    tile = groups * cells
    params = pltpu.CompilerParams(vmem_limit_bytes=VMEM_LIMIT)
    mode, rad = (lax.axis_index(axis).astype(jnp.int32).reshape(1) for axis in ("mode", "rad"))

    direct = direct_field.reshape(harms, groups, group_rows, radial)
    adjoint = adjoint_field.reshape(harms, groups, group_rows, radial)
    swap = [(0, 1), (1, 0)]
    far_direct = lax.ppermute(direct, "rad", swap)
    far_adjoint = lax.ppermute(adjoint, "rad", swap)

    sizes = (harms, blocks, width)
    depth, span = harms * LANES, blocks * LANES
    matrices = pl.pallas_call(
        functools.partial(matrix_kernel, sizes, groups),
        out_shape=[
            jax.ShapeDtypeStruct((depth, span), jnp.bfloat16),
            jax.ShapeDtypeStruct((2 * depth, span), jnp.bfloat16),
        ],
        in_specs=smem(2) + vmem(2),
        out_specs=vmem(2),
        compiler_params=params,
        name="matrices",
    )(mode, rad, direct, adjoint)
    payload_rows = 2 * fields * tile + 2 * group_rows + SLOT_ROWS
    slabs = pl.pallas_call(
        functools.partial(pack_kernel, sizes, cells),
        out_shape=[jax.ShapeDtypeStruct((payload_rows, LANES), jnp.bfloat16)] * blocks,
        in_specs=smem(1) + vmem(6),
        out_specs=vmem(blocks),
        compiler_params=params,
        name="pack",
    )(jnp.swapaxes(triad_slots, 1, 2), direct, adjoint, far_direct, far_adjoint, *matrices)
    came = moved_up(slabs, "mode")

    per_harm, own_cells = blocks // harm_devices, cells // blocks
    sizes = (harms, blocks, width, groups, slots, fields, cells, harm_devices)
    listed = (max(blocks, 8), LANES)
    derived = pltpu.VMEM((2 * fields, blocks * groups, cells, LANES), jnp.float32)
    out_rows = 2 * fields * own_cells
    sent = pl.pallas_call(
        functools.partial(triad_kernel, sizes),
        out_shape=jax.ShapeDtypeStruct(
            (blocks * harm_devices, per_harm, out_rows, LANES), jnp.float32
        ),
        in_specs=smem(1) + vmem(blocks),
        out_specs=vmem(1)[0],
        scratch_shapes=[
            pltpu.VMEM((groups, 2 * LANES, LANES), jnp.bfloat16),
            pltpu.VMEM((tile, tile), jnp.bfloat16),
            pltpu.VMEM((4, blocks * groups, cells, LANES), jnp.float32),
            derived,
            derived,
            pltpu.VMEM((blocks * slots, 2 * fields, cells, LANES), jnp.float32),
            pltpu.VMEM(listed, jnp.int32),
            pltpu.SMEM(listed, jnp.int32),
            pltpu.SemaphoreType.DMA,
        ],
        compiler_params=params,
        name="triads",
    )(mode, *came)
    owned = lax.all_to_all(sent, ("mode", "harm"), split_axis=0, concat_axis=0, tiled=True)

    result = pl.pallas_call(
        functools.partial(unpack_kernel, (blocks, harm_devices, slots, width, per_harm)),
        out_shape=jax.ShapeDtypeStruct((per_harm * slots, out_rows, LANES), jnp.float32),
        in_specs=vmem(1),
        out_specs=vmem(1)[0],
        compiler_params=params,
        name="unpack",
    )(owned)
    return result.reshape(per_harm * slots, 2, fields, own_cells, radial)


def solution(mesh):
    return jax.shard_map(
        body,
        mesh=mesh,
        in_specs=(
            P(("case", "harm"), "mode", None, None, None, "rad"),
            P(("case", "harm"), "mode", None, None, None, "rad"),
            P("mode", None, None),
        ),
        out_specs=P(("case", "harm"), None, None, "mode", "rad"),
        check_vma=False,
    )
```
